256 devices in a mesh: mod: 4 (over x), tok: 16 (over z, core), tp: 4 (over y).
Axes of the slice: x: 4, y: 4, z: 8, core: 2. Of those that a mesh axis runs over, the one named last changes fastest.
Arguments:
- hidden_in: bfloat16 [2048, 8192], P('tok', 'tp'), may hold values from -19 to 19
- spans: int32 [128, 3], replicated, may hold values from 0 to 2048, as said below
- w_qkv: bfloat16 [4, 8192, 3, 64, 128], P('mod', 'tp', None, 'tok'), may hold values from -0.088388348 to 0.088388348
- w_out: bfloat16 [4, 64, 128, 8192], P('mod', 'tok', None, 'tp'), may hold values from -0.0625 to 0.0625
Outputs:
- section_out: bfloat16 [4, 1024, 8192], P('mod', 'tok', 'tp')
The draws below stay inside these ranges and needn't reach their ends.
Inputs may be any that keep to these rules, and one draw needn't show every extreme that they name: `spans`: entries are the maximal runs of one modality, in order of start; starts and lengths are multiples of 16 and the runs cover the sequence. Unused entries have start 2048, length 0 and modality 0. Modality 0 holds exactly 1024 rows, every other modality at most that.
All inputs are finite; a program needn't handle non-finite values.
Results may differ from the reference program's by a relative error of at most 0.024.
Values may be sent and summed in bfloat16 or wider, within the bound.
A program may use at most 128 MiB of HBM per device.

```python
import jax
import jax.numpy as jnp
from jax import lax

D = 8192
HEADS = 64
HEAD_DIM = 128
MODS = 4
SEQ = 2048
CAPACITY = 1024


def draw_hidden_in(key, part):
    key = jax.random.fold_in(key, 5)
    noise_key = jax.random.fold_in(key, 0)
    values = jnp.clip(jax.random.normal(noise_key, (SEQ, D), jnp.float32), -6.0, 6.0)
    return values.astype(jnp.bfloat16)


def draw_w_qkv(key, part):
    key = jax.random.fold_in(key, 11)
    shape = (MODS, D, 3, HEADS, HEAD_DIM)
    base = jnp.clip(jax.random.normal(key, shape, jnp.float32), -6.0, 6.0) * D ** (-0.5)
    return base.astype(jnp.bfloat16)


def draw_spans(key, part):
    key = jax.random.fold_in(key, 23)
    order_key, other_key = jax.random.split(key)
    units = SEQ // 16
    order = jax.random.permutation(order_key, units)
    others = jax.random.randint(other_key, (units,), 1, MODS)
    rank = jnp.zeros((units,), jnp.int32).at[order].set(jnp.arange(units, dtype=jnp.int32))
    unit_mod = jnp.where(rank < units // 2, 0, others).astype(jnp.int32)
    flags = jnp.concatenate([jnp.ones((1,), jnp.int32), (unit_mod[1:] != unit_mod[:-1]).astype(jnp.int32)])
    run_id = jnp.cumsum(flags) - 1
    unit_ids = jnp.arange(units, dtype=jnp.int32)
    target = jnp.where(flags > 0, run_id, units).astype(jnp.int32)
    starts = jnp.full((units,), SEQ, jnp.int32).at[target].set(unit_ids * 16, mode='drop')
    modalities = jnp.zeros((units,), jnp.int32).at[target].set(unit_mod, mode='drop')
    lengths = jax.ops.segment_sum(jnp.full((units,), 16, jnp.int32), run_id, num_segments=units)
    return jnp.stack([starts, lengths, modalities], axis=1).astype(jnp.int32)


def block_scale(own_key, dims, pieces, low, top_value):
    def one(dim, parts):
        heights = jax.random.uniform(jax.random.fold_in(jax.random.fold_in(own_key, 6), dim), (parts,), jnp.float32, low / len(pieces), top_value / len(pieces))
        return jnp.repeat(jnp.exp(heights), dims[dim] // parts).reshape((-1,) + (1,) * (len(dims) - dim - 1))

    level = one(*pieces[0])
    for cut in pieces[1:]:
        level = level * one(*cut)
    return level


def bell_draw(own_key, shape, spread, limit, cuts=(), kind=jnp.bfloat16):
    gain = block_scale(own_key, shape, cuts, -0.22, 0.18) if cuts else 1.0
    drawn = jax.random.normal(own_key, shape, jnp.float32) * spread * gain
    return jnp.minimum(jnp.maximum(drawn, -limit), limit).astype(kind)


def setup_inputs(seed: int = 0) -> dict:
    splits = jax.random.split(jax.random.key(seed), 5)
    return {
        "hidden_in": draw_hidden_in(jax.random.fold_in(splits[4], 71), 0),
        "spans": draw_spans(jax.random.fold_in(splits[4], 71), 0),
        "w_qkv": draw_w_qkv(jax.random.fold_in(splits[4], 71), 0),
        "w_out": bell_draw(splits[3], (MODS, HEADS, HEAD_DIM, D), (HEADS * HEAD_DIM) ** -0.5, 0.0625, ((0, 4), (1, 16), (3, 4))),
    }


big_negative = -1.0e30


def row_modalities(spans, seq_len):
    row_ids = jnp.arange(seq_len, dtype=jnp.int32)
    ends = spans[:, 0] + spans[:, 1]
    inside = (row_ids[:, None] >= spans[None, :, 0]) & (row_ids[:, None] < ends[None, :])
    return jnp.sum(jnp.where(inside, spans[None, :, 2], 0), axis=1).astype(jnp.int32)


def modality_slots(row_modality, capacity, modality):
    seq_len = row_modality.shape[0]
    row_ids = jnp.arange(seq_len, dtype=jnp.int32)
    chosen = row_modality == modality
    slot_index = jnp.cumsum(chosen.astype(jnp.int32)) - 1
    target = jnp.where(chosen, slot_index, capacity).astype(jnp.int32)
    source = jnp.zeros((capacity,), jnp.int32).at[target].set(row_ids, mode="drop")
    live_count = jnp.sum(chosen.astype(jnp.int32))
    is_valid = jnp.arange(capacity, dtype=jnp.int32) < live_count
    return source, is_valid


def attend_head(head_triple, query_pos, key_pos, score_scale):
    query_head, key_head, value_head = head_triple
    scores = jnp.dot(query_head, key_head.T, preferred_element_type=jnp.float32) * score_scale
    allowed = key_pos[None, :] <= query_pos[:, None]
    scores = jnp.where(allowed, scores, big_negative)
    running_top = jnp.max(scores, axis=1, keepdims=True)
    weights = jnp.exp(scores - running_top)
    weight_sum = jnp.sum(weights, axis=1, keepdims=True)
    mixture = jnp.dot(weights.astype(jnp.bfloat16), value_head, preferred_element_type=jnp.float32)
    return (mixture / weight_sum).astype(jnp.bfloat16)


def reference(hidden_in, spans, w_qkv, w_out):
    row_modality = row_modalities(spans, SEQ)
    sources = []
    valids = []
    parts_qkv = []
    for modality in range(MODS):
        source, is_valid = modality_slots(row_modality, CAPACITY, modality)
        sources.append(source)
        valids.append(is_valid)
        picked = hidden_in[source]
        flattened = jnp.dot(picked, w_qkv[modality].reshape(D, 3 * HEADS * HEAD_DIM), preferred_element_type=jnp.float32)
        parts_qkv.append(flattened.astype(jnp.bfloat16).reshape(CAPACITY, 3, HEADS, HEAD_DIM))
    qkv_all = jnp.concatenate(parts_qkv, axis=0)
    query_rows = jnp.transpose(qkv_all[:, 0], (1, 0, 2))
    key_rows = jnp.transpose(qkv_all[:, 1], (1, 0, 2))
    value_rows = jnp.transpose(qkv_all[:, 2], (1, 0, 2))
    query_pos = jnp.concatenate([jnp.where(valids[i], sources[i], SEQ - 1) for i in range(MODS)]).astype(jnp.int32)
    key_pos = jnp.concatenate([jnp.where(valids[i], sources[i], SEQ) for i in range(MODS)]).astype(jnp.int32)
    score_scale = HEAD_DIM ** -0.5
    attended = lax.map(lambda triple: attend_head(triple, query_pos, key_pos, score_scale), (query_rows, key_rows, value_rows))
    outputs = []
    for modality in range(MODS):
        head_part = attended[:, modality * CAPACITY:(modality + 1) * CAPACITY]
        flattened = jnp.transpose(head_part, (1, 0, 2)).reshape(CAPACITY, HEADS * HEAD_DIM)
        projection = jnp.dot(flattened, w_out[modality].reshape(HEADS * HEAD_DIM, D), preferred_element_type=jnp.float32)
        residual = hidden_in[sources[modality]].astype(jnp.float32)
        result = jnp.where(valids[modality][:, None], residual + projection, 0.0)
        outputs.append(result.astype(jnp.bfloat16))
    return jnp.stack(outputs)
```

```python
import jax
import jax.numpy as jnp
from jax import lax
from jax.experimental import pallas as pl
from jax.experimental.pallas import tpu as pltpu
from jax.sharding import PartitionSpec as P

MESH = pl.DeviceIdType.MESH
UNIT = 16
NEG = -1e30


def remote(src, dst, send, recv, dev):
    return pltpu.make_async_remote_copy(
        src_ref=src, dst_ref=dst, send_sem=send, recv_sem=recv, device_id=dev, device_id_type=MESH
    )


def greet(devs):
    barrier = pltpu.get_barrier_semaphore()
    for dev in devs:
        pl.semaphore_signal(barrier, inc=1, device_id=dev, device_id_type=MESH)
    pl.semaphore_wait(barrier, len(devs))


def where_am_i():
    t = lax.axis_index("tok")
    return lax.axis_index("mod"), lax.div(t, 2), lax.rem(t, 2), lax.axis_index("tp")


def project_kernel(
    src_ref, hid_ref, w_ref,
    q_ref, kv_ref, res_ref,
    xg, wv, y, yc, sbuf, rbuf,
    local_sem, z_send, z_recv, x_send, x_recv, c_send, c_recv, own_sem,
    rs_send, rs_recv, g_send, g_recv, f_send, f_recv,
):
    xm, z, c, yp = where_am_i()
    half = lax.rem(xm, 2)
    zdev = [{"tok": lax.rem(z + 1, 8) * 2 + c}, {"tok": lax.rem(z + 7, 8) * 2 + c}]
    xdev = [{"mod": lax.rem(xm + 1, 4)}, {"mod": lax.rem(xm + 3, 4)}]
    ydev = [{"tp": lax.rem(yp + 1, 4)}, {"tp": lax.rem(yp + 3, 4)}]
    cdev = {"tok": z * 2 + 1 - c}

    def region(zz, cc, hh, s):
        units = pl.ds((zz * 2 + cc) * 8, 8)
        return xg.at[units, :, pl.ds(pl.multiple_of(hh * 1024 + s * 512, 512), 512)]

    def own_rows(cc):
        return xg.at[pl.ds((z * 2 + cc) * 8, 8)]

    def block_at(way, d):
        return lax.rem(z + 8 - d, 8) if way == 0 else lax.rem(z + d, 8)

    hid_copy = pltpu.make_async_copy(hid_ref, own_rows(c), local_sem.at[0])
    hid_copy.start()
    w_copy = pltpu.make_async_copy(w_ref, wv, local_sem.at[1])
    w_copy.start()
    greet(zdev + xdev + ydev + [cdev])
    hid_copy.wait()

    sent = []

    def send(src, dst, ssem, rsem, dev):
        copy = remote(src, dst, ssem, rsem, dev)
        copy.start()
        sent.append(copy)

    for s in range(2):
        for way in range(2):
            reg = region(z, c, half, s)
            send(reg, reg, z_send.at[way, 0, s], z_recv.at[way, 0, s], zdev[way])
    send(own_rows(c), own_rows(c), own_sem.at[0], own_sem.at[1], cdev)

    def multiply(zz):
        units = pl.ds(zz * 16, 16)

        def step(j, carry):
            cols = pl.ds(pl.multiple_of(j * 256, 256), 256)
            value = jnp.dot(
                xg[units].reshape(256, 2048), wv[:, cols], preferred_element_type=jnp.float32
            )
            y[units, :, cols] = value.astype(jnp.bfloat16).reshape(16, UNIT, 256)
            return carry

        lax.fori_loop(0, 6, step, 0)

    w_copy.wait()
    remote(own_rows(1 - c), own_rows(1 - c), own_sem.at[0], own_sem.at[1], cdev).wait_recv()
    multiply(z)

    events = []
    for d in range(1, 5):
        for s in range(2):
            for way in range(2):
                if d < 4 or s == way:
                    events.append((way, d, s))

    def from_x(ev):
        way, d, s = ev
        reg = region(block_at(way, d), c, 1 - half, s)
        remote(reg, reg, x_send.at[way, d - 1, s], x_recv.at[way, d - 1, s], xdev[s]).wait_recv()
        send(reg, reg, c_send.at[way, d - 1, s, 1], c_recv.at[way, d - 1, s, 1], cdev)

    def from_core(way, d):
        for s in range(2):
            w = s if d == 4 else way
            for o in range(2):
                hh = half if o == 0 else 1 - half
                reg = region(block_at(way, d), 1 - c, hh, s)
                remote(reg, reg, c_send.at[w, d - 1, s, o], c_recv.at[w, d - 1, s, o], cdev).wait_recv()

    for k, ev in enumerate(events):
        way, d, s = ev
        reg = region(block_at(way, d), c, half, s)
        remote(reg, reg, z_send.at[way, d - 1, s], z_recv.at[way, d - 1, s], zdev[way]).wait_recv()
        if d < 3 or (d == 3 and s == way):
            send(reg, reg, z_send.at[way, d, s], z_recv.at[way, d, s], zdev[way])
        send(reg, reg, x_send.at[way, d - 1, s], x_recv.at[way, d - 1, s], xdev[s])
        send(reg, reg, c_send.at[way, d - 1, s, 0], c_recv.at[way, d - 1, s, 0], cdev)
        if k >= 2:
            from_x(events[k - 2])
        if k in (5, 9):
            from_core(0, k // 4)
            multiply(block_at(0, k // 4))
        if k in (7, 11):
            from_core(1, k // 4)
            multiply(block_at(1, k // 4))
    from_x(events[-2])
    from_x(events[-1])
    for way in range(2):
        from_core(way, 3)
        multiply(block_at(way, 3))
    from_core(0, 4)
    multiply(block_at(0, 4))

    t = z * 2 + c
    for i in range(4):
        res_ref[i * UNIT:(i + 1) * UNIT, :] = xg[src_ref[t * 4 + i]]

    def compact(i, carry):
        to = pl.ds(pl.multiple_of(i * UNIT, UNIT), UNIT)
        rows = y[src_ref[i]]
        for j in range(12):
            yc[j, to, :] = rows[:, j * 128:(j + 1) * 128]
        return carry

    lax.fori_loop(0, 64, compact, 0)

    kinds = (1, 2, 0)
    turn = (1, 3)

    def rows_of(way, sub):
        return pl.ds(way * 512 + sub * 256, 256)

    def add(kind, dest, way, sub, step):
        return (
            yc[kind * 4 + dest, rows_of(way, sub), :].astype(jnp.float32)
            + rbuf[way, kind, sub, step].astype(jnp.float32)
        ).astype(jnp.bfloat16)

    def arrived(kind, way, sub, step):
        remote(
            rbuf.at[way, kind, sub, step], rbuf.at[way, kind, sub, step],
            rs_send.at[way, kind, sub, step], rs_recv.at[way, kind, sub, step], ydev[way],
        ).wait_recv()

    def hop(kind, step):
        for sub in range(2):
            for way in range(2):
                dest = lax.rem(yp + 4 * 3 - turn[way] * (step + 1), 4)
                if step == 0:
                    src = yc.at[kind * 4 + dest, rows_of(way, sub), :]
                else:
                    arrived(kind, way, sub, step - 1)
                    sbuf[way, kind, sub, step - 1] = add(kind, dest, way, sub, step - 1)
                    src = sbuf.at[way, kind, sub, step - 1]
                send(
                    src, rbuf.at[way, kind, sub, step],
                    rs_send.at[way, kind, sub, step], rs_recv.at[way, kind, sub, step], ydev[way],
                )

    def kv_rows(section, kind, way, sub):
        return kv_ref.at[kind - 1, pl.ds(section * 64 + way * 32 + sub * 16, 16)]

    def final(kind):
        for sub in range(2):
            for way in range(2):
                arrived(kind, way, sub, 2)
                value = add(kind, yp, way, sub, 2)
                if kind == 0:
                    q_ref[rows_of(way, sub), :] = value
                else:
                    reg = kv_rows(xm, kind, way, sub)
                    reg[...] = value.reshape(16, UNIT, 128)
                    for o in range(2):
                        send(
                            reg, reg, g_send.at[o, kind - 1, way, sub],
                            g_recv.at[o, kind - 1, way, sub], xdev[o],
                        )

    def spread(kind):
        for sub in range(2):
            for way in range(2):
                reg = kv_rows(lax.rem(xm + (3, 1)[way], 4), kind, way, sub)
                remote(
                    reg, reg, g_send.at[way, kind - 1, way, sub],
                    g_recv.at[way, kind - 1, way, sub], xdev[way],
                ).wait_recv()
                send(
                    reg, reg, f_send.at[kind - 1, way, sub],
                    f_recv.at[kind - 1, way, sub], xdev[way],
                )

    hop(1, 0)
    hop(1, 1)
    hop(1, 2)
    hop(2, 0)
    final(1)
    hop(2, 1)
    hop(2, 2)
    hop(0, 0)
    final(2)
    spread(1)
    hop(0, 1)
    hop(0, 2)
    spread(2)
    final(0)
    for kind in (1, 2):
        for sub in range(2):
            for way in range(2):
                reg = kv_rows(lax.rem(xm + (1, 3)[way], 4), kind, way, sub)
                remote(
                    reg, reg, g_send.at[1 - way, kind - 1, way, sub],
                    g_recv.at[1 - way, kind - 1, way, sub], xdev[1 - way],
                ).wait_recv()
                reg = kv_rows(lax.rem(xm + 2, 4), kind, way, sub)
                remote(
                    reg, reg, f_send.at[kind - 1, way, sub],
                    f_recv.at[kind - 1, way, sub], xdev[way],
                ).wait_recv()
    for copy in sent:
        copy.wait_send()


def attend_kernel(
    src_ref, slot_ref, live_ref, q_ref, kv_ref, wo_ref, res_ref,
    out_ref,
    kt, vt, heads, zown, csend, crecv, rsend, rrecv,
    h_send, h_recv, c_send_sem, c_recv_sem, r_send_sem, r_recv_sem,
):
    xm, z, c, yp = where_am_i()
    zdev = [{"tok": lax.rem(z + 1, 8) * 2 + c}, {"tok": lax.rem(z + 7, 8) * 2 + c}]
    ydev = [{"tp": lax.rem(yp + k, 4)} for k in (1, 2, 3)]
    cdev = {"tok": z * 2 + 1 - c}
    greet(zdev + ydev + [cdev])

    def order_keys(u, carry):
        to = pl.ds(pl.multiple_of(u * UNIT, UNIT), UNIT)
        unit = slot_ref[u]
        kt[to, :] = kv_ref[0, unit]
        vt[to, :] = kv_ref[1, unit]
        return carry

    lax.fori_loop(0, 128, order_keys, 0)

    dests = [lax.rem(z + k, 8) for k in (4, 3, 5, 2, 6, 1, 7, 0)]
    sent = []

    def send(src, dst, ssem, rsem, dev):
        copy = remote(src, dst, ssem, rsem, dev)
        copy.start()
        sent.append(copy)

    def my_cols(p):
        return pl.ds(pl.multiple_of(p * 128, 128), 128)

    def attend(i):
        d = dests[i]
        query = q_ref[pl.ds(pl.multiple_of(d * 128, 128), 128), :]
        scores = lax.dot_general(
            query, kt[...], (((1,), (1,)), ((), ())), preferred_element_type=jnp.float32
        ) * (128 ** -0.5)
        base = jnp.concatenate(
            [jnp.full((UNIT, 1), src_ref[d * 8 + k] * UNIT, jnp.int32) for k in range(8)], axis=0
        )
        row = lax.broadcasted_iota(jnp.int32, (128, 1), 0)
        pos = base + lax.rem(row, UNIT)
        key = lax.broadcasted_iota(jnp.int32, (128, 2048), 1)
        scores = jnp.where(key <= pos, scores, NEG)
        top = jnp.max(scores, axis=1, keepdims=True)
        weights = jnp.exp(scores - top)
        total = jnp.sum(weights, axis=1, keepdims=True)
        mixed = jnp.dot(weights.astype(jnp.bfloat16), vt[...], preferred_element_type=jnp.float32)
        heads[i, :, my_cols(yp)] = (mixed / total).astype(jnp.bfloat16)
        mine = heads.at[i, :, my_cols(yp)]
        for k in range(3):
            send(mine, mine, h_send.at[i, k], h_recv.at[i, k], ydev[k])

    def project(i):
        for k in range(3):
            other = heads.at[i, :, my_cols(lax.rem(yp + 3 - k, 4))]
            remote(other, other, h_send.at[i, k], h_recv.at[i, k], ydev[k]).wait_recv()
        def part(j, carry):
            cols = pl.ds(pl.multiple_of(j * 512, 512), 512)
            value = jnp.dot(heads[i], wo_ref[:, cols], preferred_element_type=jnp.float32)
            first = value[:64]
            second = value[64:]
            zown[i, :, cols] = jnp.where(c == 0, first, second)
            csend[i, :, cols] = jnp.where(c == 0, second, first).astype(jnp.bfloat16)
            return carry

        lax.fori_loop(0, 4, part, 0)
        send(csend.at[i], crecv.at[i], c_send_sem.at[i], c_recv_sem.at[i], cdev)

    top_of = {(0, 0): 3, (0, 1): 4, (1, 0): 4, (1, 1): 3}

    def ring(way, dist, part):
        i = {4: 0, 3: 1, 2: 3, 1: 5}[dist] + (1 if way == 1 and dist < 4 else 0)
        cols = slice(part * 1024, part * 1024 + 1024)
        value = zown[i, :, cols] + crecv[i, :, cols].astype(jnp.float32)
        if dist < top_of[(way, part)]:
            came = rrecv.at[way, dist, part]
            remote(
                came, came, r_send_sem.at[way, dist, part], r_recv_sem.at[way, dist, part], zdev[way]
            ).wait_recv()
            value = value + came[...].astype(jnp.float32)
        rsend[way, dist - 1, part] = value.astype(jnp.bfloat16)
        send(
            rsend.at[way, dist - 1, part], rrecv.at[way, dist - 1, part],
            r_send_sem.at[way, dist - 1, part], r_recv_sem.at[way, dist - 1, part], zdev[way],
        )

    def core_sum(i):
        remote(crecv.at[i], crecv.at[i], c_send_sem.at[i], c_recv_sem.at[i], cdev).wait_recv()

    def pass_on(i):
        core_sum(i)
        if i == 0:
            ring(1, 4, 0)
            ring(0, 4, 1)
        elif i < 7:
            way = (i - 1) % 2
            dist = 3 - (i - 1) // 2
            for part in ((0, 1) if way == 0 else (1, 0)):
                ring(way, dist, part)

    for i in range(8):
        attend(i)
        if i >= 1:
            project(i - 1)
        if i >= 2:
            pass_on(i - 2)
    project(7)
    pass_on(6)
    core_sum(7)

    t = z * 2 + c
    live_rows = live_ref[0] * UNIT
    for part in range(2):
        cols = slice(part * 1024, part * 1024 + 1024)
        value = zown[7, :, cols] + crecv[7, :, cols].astype(jnp.float32)
        for way in range(2):
            came = rrecv.at[way, 0, part]
            remote(
                came, came, r_send_sem.at[way, 0, part], r_recv_sem.at[way, 0, part], zdev[way]
            ).wait_recv()
            value = value + came[...].astype(jnp.float32)
        value = value + res_ref[:, cols].astype(jnp.float32)
        row = lax.broadcasted_iota(jnp.int32, (64, 1024), 0) + t * 64
        out_ref[:, cols] = jnp.where(row < live_rows, value, 0.0).astype(jnp.bfloat16)
    for copy in sent:
        copy.wait_send()


def plan(spans):
    units = spans.shape[0]
    ids = jnp.arange(units, dtype=jnp.int32)
    at = ids * UNIT
    ends = spans[:, 0] + spans[:, 1]
    inside = (at[:, None] >= spans[None, :, 0]) & (at[:, None] < ends[None, :])
    unit_mod = jnp.sum(jnp.where(inside, spans[None, :, 2], 0), axis=1)
    before = (unit_mod[:, None] == unit_mod[None, :]) & (ids[None, :] < ids[:, None])
    rank = jnp.sum(before.astype(jnp.int32), axis=1)
    slot = unit_mod * 64 + rank
    mine = unit_mod == lax.axis_index("mod")
    here = mine[None, :] & (rank[None, :] == jnp.arange(64, dtype=jnp.int32)[:, None])
    src = jnp.sum(jnp.where(here, ids[None, :], 0), axis=1)
    live = jnp.sum(mine.astype(jnp.int32)).reshape(1)
    return src, slot, live


def local(hidden_in, spans, w_qkv, w_out):
    src, slot, live = plan(spans)
    w = w_qkv[0].reshape(2048, 1536)
    wo = w_out.reshape(512, 2048)
    bf = jnp.bfloat16
    dma = pltpu.SemaphoreType.DMA
    vmem = pl.BlockSpec(memory_space=pltpu.VMEM)
    smem = pl.BlockSpec(memory_space=pltpu.SMEM)
    anyw = pl.BlockSpec(memory_space=pl.ANY)
    q, kv, res = pl.pallas_call(
        project_kernel,
        out_shape=(
            jax.ShapeDtypeStruct((1024, 128), bf),
            jax.ShapeDtypeStruct((2, 256, UNIT, 128), bf),
            jax.ShapeDtypeStruct((64, 2048), bf),
        ),
        in_specs=[smem, anyw, anyw],
        out_specs=(vmem, vmem, vmem),
        scratch_shapes=[
            pltpu.VMEM((128, UNIT, 2048), bf),
            pltpu.VMEM((2048, 1536), bf),
            pltpu.VMEM((128, UNIT, 1536), bf),
            pltpu.VMEM((12, 1024, 128), bf),
            pltpu.VMEM((2, 3, 2, 2, 256, 128), bf),
            pltpu.VMEM((2, 3, 2, 3, 256, 128), bf),
            dma((2,)),
            dma((2, 4, 2)), dma((2, 4, 2)),
            dma((2, 4, 2)), dma((2, 4, 2)),
            dma((2, 4, 2, 2)), dma((2, 4, 2, 2)),
            dma((2,)),
            dma((2, 3, 2, 3)), dma((2, 3, 2, 3)),
            dma((2, 2, 2, 2)), dma((2, 2, 2, 2)),
            dma((2, 2, 2)), dma((2, 2, 2)),
        ],
        compiler_params=pltpu.CompilerParams(
            collective_id=1, has_side_effects=True, vmem_limit_bytes=56 * 1024 * 1024
        ),
        name="project",
    )(src, hidden_in.reshape(8, UNIT, 2048), w)
    out = pl.pallas_call(
        attend_kernel,
        out_shape=jax.ShapeDtypeStruct((64, 2048), bf),
        in_specs=[smem, smem, smem, vmem, vmem, vmem, vmem],
        out_specs=vmem,
        scratch_shapes=[
            pltpu.VMEM((2048, 128), bf),
            pltpu.VMEM((2048, 128), bf),
            pltpu.VMEM((8, 128, 512), bf),
            pltpu.VMEM((8, 64, 2048), jnp.float32),
            pltpu.VMEM((8, 64, 2048), bf),
            pltpu.VMEM((8, 64, 2048), bf),
            pltpu.VMEM((2, 4, 2, 64, 1024), bf),
            pltpu.VMEM((2, 4, 2, 64, 1024), bf),
            dma((8, 3)), dma((8, 3)),
            dma((8,)), dma((8,)),
            dma((2, 4, 2)), dma((2, 4, 2)),
        ],
        compiler_params=pltpu.CompilerParams(
            collective_id=2, has_side_effects=True, vmem_limit_bytes=56 * 1024 * 1024
        ),
        name="attend",
    )(src, slot, live, q, kv, wo, res)
    return out[None]


def solution(mesh):
    in_specs = (P("tok", "tp"), P(), P("mod", "tp", None, "tok", None), P("mod", "tok", None, "tp"))
    out_specs = P("mod", "tok", "tp")
    return jax.shard_map(local, mesh=mesh, in_specs=in_specs, out_specs=out_specs, check_vma=False)
```

```python
import jax
import jax.numpy as jnp
from jax import lax
from jax.experimental import pallas as pl
from jax.experimental.pallas import tpu as pltpu
from jax.sharding import PartitionSpec as P

MESH = pl.DeviceIdType.MESH
UNIT = 16
NEG = -1e30


def remote(src, dst, send, recv, dev):
    return pltpu.make_async_remote_copy(
        src_ref=src, dst_ref=dst, send_sem=send, recv_sem=recv, device_id=dev, device_id_type=MESH
    )


def greet(devs):
    barrier = pltpu.get_barrier_semaphore()
    for dev in devs:
        pl.semaphore_signal(barrier, inc=1, device_id=dev, device_id_type=MESH)
    pl.semaphore_wait(barrier, len(devs))


def where_am_i():
    t = lax.axis_index("tok")
    return lax.axis_index("mod"), lax.div(t, 2), lax.rem(t, 2), lax.axis_index("tp")


def project_kernel(
    src_ref, hid_ref, w_ref,
    q_ref, kv_ref, res_ref,
    xg, wr, wf, wv, xs, yc, sbuf, rbuf,
    local_sem, z_send, z_recv, x_send, x_recv, c_send, c_recv, own_sem,
    rs_send, rs_recv, g_send, g_recv, f_send, f_recv,
):
    xm, z, c, yp = where_am_i()
    half = lax.rem(xm, 2)
    zdev = [{"tok": lax.rem(z + 1, 8) * 2 + c}, {"tok": lax.rem(z + 7, 8) * 2 + c}]
    xdev = [{"mod": lax.rem(xm + 1, 4)}, {"mod": lax.rem(xm + 3, 4)}]
    ydev = [{"tp": lax.rem(yp + 1, 4)}, {"tp": lax.rem(yp + 3, 4)}]
    cdev = {"tok": z * 2 + 1 - c}

    def region(zz, cc, hh, s):
        units = pl.ds((zz * 2 + cc) * 8, 8)
        return xg.at[units, :, pl.ds(pl.multiple_of(hh * 1024 + s * 512, 512), 512)]

    def own_rows(cc):
        return xg.at[pl.ds((z * 2 + cc) * 8, 8)]

    def block_at(way, d):
        return lax.rem(z + 8 - d, 8) if way == 0 else lax.rem(z + d, 8)

    hid_copy = pltpu.make_async_copy(hid_ref, own_rows(c), local_sem.at[0])
    hid_copy.start()
    w_copy = pltpu.make_async_copy(w_ref, wr, local_sem.at[1])
    w_copy.start()
    greet(zdev + xdev + ydev + [cdev])
    hid_copy.wait()

    sent = []

    def send(src, dst, ssem, rsem, dev):
        copy = remote(src, dst, ssem, rsem, dev)
        copy.start()
        sent.append(copy)

    for s in range(2):
        for way in range(2):
            reg = region(z, c, half, s)
            send(reg, reg, z_send.at[way, 0, s], z_recv.at[way, 0, s], zdev[way])
    send(own_rows(c), own_rows(c), own_sem.at[0], own_sem.at[1], cdev)

    def lay_out(first, count):
        def step(i, carry):
            at = pl.multiple_of((first + i) * 32, 32)
            wf[...] = wr[pl.ds(pl.multiple_of(at * 12, 384), 384), :].astype(jnp.float32)
            for kind in range(3):
                for h in range(4):
                    rows = wf[pl.ds(kind * 4 + h, 32, stride=12), :]
                    wv[kind, pl.ds(at, 32), h * 128:(h + 1) * 128] = rows.astype(jnp.bfloat16)
            return carry

        lax.fori_loop(0, count, step, 0)

    w_copy.wait()
    lay_out(0, 8)

    events = []
    for d in range(1, 5):
        for s in range(2):
            for way in range(2):
                if d < 4 or s == way:
                    events.append((way, d, s))

    def from_x(ev):
        way, d, s = ev
        reg = region(block_at(way, d), c, 1 - half, s)
        remote(reg, reg, x_send.at[way, d - 1, s], x_recv.at[way, d - 1, s], xdev[s]).wait_recv()
        send(reg, reg, c_send.at[way, d - 1, s, 1], c_recv.at[way, d - 1, s, 1], cdev)

    def from_core(ev):
        way, d, s = ev
        for o in range(2):
            hh = half if o == 0 else 1 - half
            reg = region(block_at(way, d), 1 - c, hh, s)
            remote(reg, reg, c_send.at[way, d - 1, s, o], c_recv.at[way, d - 1, s, o], cdev).wait_recv()

    for k, ev in enumerate(events):
        way, d, s = ev
        reg = region(block_at(way, d), c, half, s)
        remote(reg, reg, z_send.at[way, d - 1, s], z_recv.at[way, d - 1, s], zdev[way]).wait_recv()
        if d < 3 or (d == 3 and s == way):
            send(reg, reg, z_send.at[way, d, s], z_recv.at[way, d, s], zdev[way])
        send(reg, reg, x_send.at[way, d - 1, s], x_recv.at[way, d - 1, s], xdev[s])
        send(reg, reg, c_send.at[way, d - 1, s, 0], c_recv.at[way, d - 1, s, 0], cdev)
        if k >= 4:
            from_x(events[k - 4])
        lay_out(8 + k * 4, 4)
    for ev in events[-4:]:
        from_x(ev)
    remote(own_rows(1 - c), own_rows(1 - c), own_sem.at[0], own_sem.at[1], cdev).wait_recv()
    for ev in events:
        from_core(ev)

    def compact(i, carry):
        xs[pl.ds(pl.multiple_of(i * UNIT, UNIT), UNIT), :] = xg[src_ref[i]]
        return carry

    lax.fori_loop(0, 64, compact, 0)
    t = z * 2 + c
    res_ref[...] = xs[pl.ds(pl.multiple_of(t * 64, 64), 64), :]

    def multiply(kind):
        for way in range(2):
            rows = slice(way * 512, way * 512 + 512)
            for n in range(2):
                value = jnp.dot(
                    xs[rows, :], wv[kind, :, n * 256:(n + 1) * 256],
                    preferred_element_type=jnp.float32,
                ).astype(jnp.bfloat16)
                yc[kind * 4 + n * 2, rows, :] = value[:, :128]
                yc[kind * 4 + n * 2 + 1, rows, :] = value[:, 128:]

    turn = (1, 3)

    def rows_of(way, sub):
        return pl.ds(way * 512 + sub * 256, 256)

    def add(kind, dest, way, sub, step):
        return (
            yc[kind * 4 + dest, rows_of(way, sub), :].astype(jnp.float32)
            + rbuf[way, kind, sub, step].astype(jnp.float32)
        ).astype(jnp.bfloat16)

    def arrived(kind, way, sub, step):
        remote(
            rbuf.at[way, kind, sub, step], rbuf.at[way, kind, sub, step],
            rs_send.at[way, kind, sub, step], rs_recv.at[way, kind, sub, step], ydev[way],
        ).wait_recv()

    def hop(kind, step, sub):
        for way in range(2):
            dest = lax.rem(yp + 4 * 3 - turn[way] * (step + 1), 4)
            if step == 0:
                src = yc.at[kind * 4 + dest, rows_of(way, sub), :]
            else:
                arrived(kind, way, sub, step - 1)
                sbuf[way, kind, sub, step - 1] = add(kind, dest, way, sub, step - 1)
                src = sbuf.at[way, kind, sub, step - 1]
            send(
                src, rbuf.at[way, kind, sub, step],
                rs_send.at[way, kind, sub, step], rs_recv.at[way, kind, sub, step], ydev[way],
            )

    def kv_rows(section, kind, way, sub):
        return kv_ref.at[kind - 1, pl.ds(section * 64 + way * 32 + sub * 16, 16)]

    def final(kind, sub):
        for way in range(2):
            arrived(kind, way, sub, 2)
            value = add(kind, yp, way, sub, 2)
            if kind == 0:
                q_ref[rows_of(way, sub), :] = value
            else:
                reg = kv_rows(xm, kind, way, sub)
                reg[...] = value.reshape(16, UNIT, 128)
                for o in range(2):
                    send(
                        reg, reg, g_send.at[o, kind - 1, way, sub],
                        g_recv.at[o, kind - 1, way, sub], xdev[o],
                    )

    def spread(kind, sub):
        for way in range(2):
            reg = kv_rows(lax.rem(xm + (3, 1)[way], 4), kind, way, sub)
            remote(
                reg, reg, g_send.at[way, kind - 1, way, sub],
                g_recv.at[way, kind - 1, way, sub], xdev[way],
            ).wait_recv()
            send(
                reg, reg, f_send.at[kind - 1, way, sub],
                f_recv.at[kind - 1, way, sub], xdev[way],
            )

    K, V, Q = 1, 2, 0
    multiply(K)
    hop(K, 0, 0)
    hop(K, 0, 1)
    multiply(V)
    hop(V, 0, 0)
    multiply(Q)
    hop(K, 1, 0)
    hop(K, 1, 1)
    hop(V, 0, 1)
    hop(K, 2, 0)
    hop(K, 2, 1)
    hop(V, 1, 0)
    hop(V, 1, 1)
    final(K, 0)
    hop(Q, 0, 0)
    final(K, 1)
    hop(V, 2, 0)
    hop(V, 2, 1)
    spread(K, 0)
    hop(Q, 0, 1)
    hop(Q, 1, 0)
    final(V, 0)
    spread(K, 1)
    final(V, 1)
    hop(Q, 1, 1)
    hop(Q, 2, 0)
    hop(Q, 2, 1)
    spread(V, 0)
    spread(V, 1)
    final(Q, 0)
    final(Q, 1)
    for kind in (1, 2):
        for sub in range(2):
            for way in range(2):
                reg = kv_rows(lax.rem(xm + (1, 3)[way], 4), kind, way, sub)
                remote(
                    reg, reg, g_send.at[1 - way, kind - 1, way, sub],
                    g_recv.at[1 - way, kind - 1, way, sub], xdev[1 - way],
                ).wait_recv()
                reg = kv_rows(lax.rem(xm + 2, 4), kind, way, sub)
                remote(
                    reg, reg, f_send.at[kind - 1, way, sub],
                    f_recv.at[kind - 1, way, sub], xdev[way],
                ).wait_recv()
    for copy in sent:
        copy.wait_send()


def attend_kernel(
    src_ref, slot_ref, live_ref, q_ref, kv_ref, wo_ref, res_ref,
    out_ref,
    kt, vt, heads, zown, csend, crecv, rsend, rrecv,
    h_send, h_recv, c_send_sem, c_recv_sem, r_send_sem, r_recv_sem,
):
    xm, z, c, yp = where_am_i()
    zdev = [{"tok": lax.rem(z + 1, 8) * 2 + c}, {"tok": lax.rem(z + 7, 8) * 2 + c}]
    ydev = [{"tp": lax.rem(yp + k, 4)} for k in (1, 2, 3)]
    cdev = {"tok": z * 2 + 1 - c}
    greet(zdev + ydev + [cdev])

    def order_keys(u, carry):
        to = pl.ds(pl.multiple_of(u * UNIT, UNIT), UNIT)
        unit = slot_ref[u]
        kt[to, :] = kv_ref[0, unit]
        vt[to, :] = kv_ref[1, unit]
        return carry

    lax.fori_loop(0, 128, order_keys, 0)

    dests = [lax.rem(z + k, 8) for k in (4, 3, 5, 2, 6, 1, 7, 0)]
    sent = []

    def send(src, dst, ssem, rsem, dev):
        copy = remote(src, dst, ssem, rsem, dev)
        copy.start()
        sent.append(copy)

    def my_cols(p):
        return pl.ds(pl.multiple_of(p * 128, 128), 128)

    def attend(i):
        d = dests[i]
        query = q_ref[pl.ds(pl.multiple_of(d * 128, 128), 128), :]
        scores = lax.dot_general(
            query, kt[...], (((1,), (1,)), ((), ())), preferred_element_type=jnp.float32
        ) * (128 ** -0.5)
        base = jnp.concatenate(
            [jnp.full((UNIT, 1), src_ref[d * 8 + k] * UNIT, jnp.int32) for k in range(8)], axis=0
        )
        row = lax.broadcasted_iota(jnp.int32, (128, 1), 0)
        pos = base + lax.rem(row, UNIT)
        key = lax.broadcasted_iota(jnp.int32, (128, 2048), 1)
        scores = jnp.where(key <= pos, scores, NEG)
        top = jnp.max(scores, axis=1, keepdims=True)
        weights = jnp.exp(scores - top)
        total = jnp.sum(weights, axis=1, keepdims=True)
        mixed = jnp.dot(weights.astype(jnp.bfloat16), vt[...], preferred_element_type=jnp.float32)
        heads[i, :, my_cols(yp)] = (mixed / total).astype(jnp.bfloat16)
        mine = heads.at[i, :, my_cols(yp)]
        for k in range(3):
            send(mine, mine, h_send.at[i, k], h_recv.at[i, k], ydev[k])

    def project(i):
        for k in range(3):
            other = heads.at[i, :, my_cols(lax.rem(yp + 3 - k, 4))]
            remote(other, other, h_send.at[i, k], h_recv.at[i, k], ydev[k]).wait_recv()
        def part(j, carry):
            cols = pl.ds(pl.multiple_of(j * 512, 512), 512)
            value = jnp.dot(heads[i], wo_ref[:, cols], preferred_element_type=jnp.float32)
            first = value[:64]
            second = value[64:]
            zown[i, :, cols] = jnp.where(c == 0, first, second)
            csend[i, :, cols] = jnp.where(c == 0, second, first).astype(jnp.bfloat16)
            return carry

        lax.fori_loop(0, 4, part, 0)
        send(csend.at[i], crecv.at[i], c_send_sem.at[i], c_recv_sem.at[i], cdev)

    top_of = {(0, 0): 3, (0, 1): 4, (1, 0): 4, (1, 1): 3}

    def ring(way, dist, part):
        i = {4: 0, 3: 1, 2: 3, 1: 5}[dist] + (1 if way == 1 and dist < 4 else 0)
        cols = slice(part * 1024, part * 1024 + 1024)
        value = zown[i, :, cols] + crecv[i, :, cols].astype(jnp.float32)
        if dist < top_of[(way, part)]:
            came = rrecv.at[way, dist, part]
            remote(
                came, came, r_send_sem.at[way, dist, part], r_recv_sem.at[way, dist, part], zdev[way]
            ).wait_recv()
            value = value + came[...].astype(jnp.float32)
        rsend[way, dist - 1, part] = value.astype(jnp.bfloat16)
        send(
            rsend.at[way, dist - 1, part], rrecv.at[way, dist - 1, part],
            r_send_sem.at[way, dist - 1, part], r_recv_sem.at[way, dist - 1, part], zdev[way],
        )

    def core_sum(i):
        remote(crecv.at[i], crecv.at[i], c_send_sem.at[i], c_recv_sem.at[i], cdev).wait_recv()

    def pass_on(i):
        core_sum(i)
        if i == 0:
            ring(1, 4, 0)
            ring(0, 4, 1)
        elif i < 7:
            way = (i - 1) % 2
            dist = 3 - (i - 1) // 2
            for part in ((0, 1) if way == 0 else (1, 0)):
                ring(way, dist, part)

    for i in range(8):
        attend(i)
        if i >= 1:
            project(i - 1)
        if i >= 2:
            pass_on(i - 2)
    project(7)
    pass_on(6)
    core_sum(7)

    t = z * 2 + c
    live_rows = live_ref[0] * UNIT
    for part in range(2):
        cols = slice(part * 1024, part * 1024 + 1024)
        value = zown[7, :, cols] + crecv[7, :, cols].astype(jnp.float32)
        for way in range(2):
            came = rrecv.at[way, 0, part]
            remote(
                came, came, r_send_sem.at[way, 0, part], r_recv_sem.at[way, 0, part], zdev[way]
            ).wait_recv()
            value = value + came[...].astype(jnp.float32)
        value = value + res_ref[:, cols].astype(jnp.float32)
        row = lax.broadcasted_iota(jnp.int32, (64, 1024), 0) + t * 64
        out_ref[:, cols] = jnp.where(row < live_rows, value, 0.0).astype(jnp.bfloat16)
    for copy in sent:
        copy.wait_send()


def plan(spans):
    units = spans.shape[0]
    ids = jnp.arange(units, dtype=jnp.int32)
    at = ids * UNIT
    ends = spans[:, 0] + spans[:, 1]
    inside = (at[:, None] >= spans[None, :, 0]) & (at[:, None] < ends[None, :])
    unit_mod = jnp.sum(jnp.where(inside, spans[None, :, 2], 0), axis=1)
    before = (unit_mod[:, None] == unit_mod[None, :]) & (ids[None, :] < ids[:, None])
    rank = jnp.sum(before.astype(jnp.int32), axis=1)
    slot = unit_mod * 64 + rank
    mine = unit_mod == lax.axis_index("mod")
    here = mine[None, :] & (rank[None, :] == jnp.arange(64, dtype=jnp.int32)[:, None])
    src = jnp.sum(jnp.where(here, ids[None, :], 0), axis=1)
    live = jnp.sum(mine.astype(jnp.int32)).reshape(1)
    return src, slot, live


def local(hidden_in, spans, w_qkv, w_out):
    src, slot, live = plan(spans)
    w = w_qkv.reshape(24576, 128)
    wo = w_out.reshape(512, 2048)
    bf = jnp.bfloat16
    dma = pltpu.SemaphoreType.DMA
    vmem = pl.BlockSpec(memory_space=pltpu.VMEM)
    smem = pl.BlockSpec(memory_space=pltpu.SMEM)
    anyw = pl.BlockSpec(memory_space=pl.ANY)
    q, kv, res = pl.pallas_call(
        project_kernel,
        out_shape=(
            jax.ShapeDtypeStruct((1024, 128), bf),
            jax.ShapeDtypeStruct((2, 256, UNIT, 128), bf),
            jax.ShapeDtypeStruct((64, 2048), bf),
        ),
        in_specs=[smem, anyw, anyw],
        out_specs=(vmem, vmem, vmem),
        scratch_shapes=[
            pltpu.VMEM((128, UNIT, 2048), bf),
            pltpu.VMEM((24576, 128), bf),
            pltpu.VMEM((384, 128), jnp.float32),
            pltpu.VMEM((3, 2048, 512), bf),
            pltpu.VMEM((1024, 2048), bf),
            pltpu.VMEM((12, 1024, 128), bf),
            pltpu.VMEM((2, 3, 2, 2, 256, 128), bf),
            pltpu.VMEM((2, 3, 2, 3, 256, 128), bf),
            dma((2,)),
            dma((2, 4, 2)), dma((2, 4, 2)),
            dma((2, 4, 2)), dma((2, 4, 2)),
            dma((2, 4, 2, 2)), dma((2, 4, 2, 2)),
            dma((2,)),
            dma((2, 3, 2, 3)), dma((2, 3, 2, 3)),
            dma((2, 2, 2, 2)), dma((2, 2, 2, 2)),
            dma((2, 2, 2)), dma((2, 2, 2)),
        ],
        compiler_params=pltpu.CompilerParams(
            collective_id=1, has_side_effects=True, vmem_limit_bytes=56 * 1024 * 1024
        ),
        name="project",
    )(src, hidden_in.reshape(8, UNIT, 2048), w)
    out = pl.pallas_call(
        attend_kernel,
        out_shape=jax.ShapeDtypeStruct((64, 2048), bf),
        in_specs=[smem, smem, smem, vmem, vmem, vmem, vmem],
        out_specs=vmem,
        scratch_shapes=[
            pltpu.VMEM((2048, 128), bf),
            pltpu.VMEM((2048, 128), bf),
            pltpu.VMEM((8, 128, 512), bf),
            pltpu.VMEM((8, 64, 2048), jnp.float32),
            pltpu.VMEM((8, 64, 2048), bf),
            pltpu.VMEM((8, 64, 2048), bf),
            pltpu.VMEM((2, 4, 2, 64, 1024), bf),
            pltpu.VMEM((2, 4, 2, 64, 1024), bf),
            dma((8, 3)), dma((8, 3)),
            dma((8,)), dma((8,)),
            dma((2, 4, 2)), dma((2, 4, 2)),
        ],
        compiler_params=pltpu.CompilerParams(
            collective_id=2, has_side_effects=True, vmem_limit_bytes=56 * 1024 * 1024
        ),
        name="attend",
    )(src, slot, live, q, kv, wo, res)
    return out[None]


def solution(mesh):
    in_specs = (P("tok", "tp"), P(), P("mod", "tp", None, "tok", None), P("mod", "tok", None, "tp"))
    out_specs = P("mod", "tok", "tp")
    return jax.shard_map(local, mesh=mesh, in_specs=in_specs, out_specs=out_specs, check_vma=False)
```

```python
import jax
import jax.numpy as jnp
from jax import lax
from jax.experimental import pallas as pl
from jax.experimental.pallas import tpu as pltpu
from jax.sharding import PartitionSpec as P

MESH = pl.DeviceIdType.MESH
UNIT = 16
NEG = -1e30


def remote(src, dst, send, recv, dev):
    return pltpu.make_async_remote_copy(
        src_ref=src, dst_ref=dst, send_sem=send, recv_sem=recv, device_id=dev, device_id_type=MESH
    )


def greet(devs):
    barrier = pltpu.get_barrier_semaphore()
    for dev in devs:
        pl.semaphore_signal(barrier, inc=1, device_id=dev, device_id_type=MESH)
    pl.semaphore_wait(barrier, len(devs))


def where_am_i():
    t = lax.axis_index("tok")
    return lax.axis_index("mod"), lax.div(t, 2), lax.rem(t, 2), lax.axis_index("tp")


SUBS = 4
PIECE = 1024 // SUBS
ROWS = 512 // SUBS


def make_plan(spans_ref, planv, me):
    down = lax.broadcasted_iota(jnp.int32, (128, 128), 0)
    across = lax.broadcasted_iota(jnp.int32, (128, 128), 1)
    eye = down == across

    def column(row):
        return jnp.sum(jnp.where(eye, row, 0), axis=1, keepdims=True)

    start = spans_ref[0:1, :]
    first = column(start)
    end = column(start + spans_ref[1:2, :])
    kind = column(spans_ref[2:3, :])
    at = across * UNIT
    inside = (at >= first) & (at < end)
    unit_mod = jnp.sum(jnp.where(inside, kind, 0), axis=0, keepdims=True)
    mod_col = column(unit_mod)
    before = (mod_col == unit_mod) & (down < across)
    rank = jnp.sum(jnp.where(before, 1, 0), axis=0, keepdims=True)
    mine = (mod_col == me) & (column(rank) == across)
    planv[0:1, :] = unit_mod * 64 + rank
    planv[1:2, :] = jnp.sum(jnp.where(mine, down, 0), axis=0, keepdims=True)
    live = jnp.sum(jnp.where(unit_mod == me, 1, 0), axis=1, keepdims=True)
    planv[2:3, :] = jnp.broadcast_to(live, (1, 128))


def block_kernel(
    spans_ref, hid_ref, w_ref, wo_ref,
    out_ref,
    planv, plans, xg, wr, wf, wv, wo, xs, yc, sbuf, rbuf, qs, kv,
    kt, vt, heads, zown, csend, crecv, rsend, rrecv,
    local_sem, z_send, z_recv, x_send, x_recv, c_send, c_recv, own_sem,
    rs_send, rs_recv, g_send, g_recv, f_send, f_recv,
    h_send, h_recv, p_send, p_recv, r_send, r_recv,
):
    xm, z, c, yp = where_am_i()
    t = z * 2 + c
    half = lax.rem(xm, 2)
    zdev = [{"tok": lax.rem(z + 1, 8) * 2 + c}, {"tok": lax.rem(z + 7, 8) * 2 + c}]
    xdev = [{"mod": lax.rem(xm + 1, 4)}, {"mod": lax.rem(xm + 3, 4)}]
    ydev = [{"tp": lax.rem(yp + 1, 4)}, {"tp": lax.rem(yp + 3, 4)}]
    opposite = {"tp": lax.rem(yp + 2, 4)}
    cdev = {"tok": z * 2 + 1 - c}

    def region(zz, cc, hh, s):
        units = pl.ds((zz * 2 + cc) * 8, 8)
        return xg.at[units, :, pl.ds(pl.multiple_of(hh * 1024 + s * PIECE, PIECE), PIECE)]

    def own_rows(cc):
        return xg.at[pl.ds((z * 2 + cc) * 8, 8)]

    def block_at(way, d):
        return lax.rem(z + 8 - d, 8) if way == 0 else lax.rem(z + d, 8)

    hid_copy = pltpu.make_async_copy(hid_ref, own_rows(c), local_sem.at[0])
    hid_copy.start()
    w_copy = pltpu.make_async_copy(w_ref, wr, local_sem.at[1])
    w_copy.start()
    wo_copy = pltpu.make_async_copy(wo_ref, wo, local_sem.at[2])
    wo_copy.start()
    greet(zdev + xdev + ydev + [opposite, cdev])
    hid_copy.wait()

    sent = []

    def send(src, dst, ssem, rsem, dev):
        copy = remote(src, dst, ssem, rsem, dev)
        copy.start()
        sent.append(copy)

    for s in range(SUBS):
        for way in range(2):
            reg = region(z, c, half, s)
            send(reg, reg, z_send.at[way, 0, s], z_recv.at[way, 0, s], zdev[way])
    send(own_rows(c), own_rows(c), own_sem.at[0], own_sem.at[1], cdev)

    make_plan(spans_ref, planv, xm)
    plan_copy = pltpu.make_async_copy(planv, plans, local_sem.at[3])
    plan_copy.start()

    def lay_out(first, count):
        def step(i, carry):
            at = pl.multiple_of((first + i) * 32, 32)
            wf[...] = wr[pl.ds(pl.multiple_of(at * 12, 384), 384), :].astype(jnp.float32)
            for j in range(12):
                rows = wf[pl.ds(j, 32, stride=12), :]
                wv[j, pl.ds(at, 32), :] = rows.astype(jnp.bfloat16)
            return carry

        lax.fori_loop(0, count, step, 0)

    events = []
    for d in range(1, 5):
        for s in range(SUBS):
            for way in range(2):
                if d < 4 or s // (SUBS // 2) == way:
                    events.append((way, d, s))
    events[-SUBS:] = [(s // (SUBS // 2), 4, s) for k in range(SUBS // 2) for s in (k, k + SUBS // 2)]

    def from_x(ev):
        way, d, s = ev
        reg = region(block_at(way, d), c, 1 - half, s)
        remote(reg, reg, x_send.at[way, d - 1, s], x_recv.at[way, d - 1, s], xdev[s % 2]).wait_recv()
        send(reg, reg, c_send.at[way, d - 1, s, 1], c_recv.at[way, d - 1, s, 1], cdev)

    def from_core(ev):
        way, d, s = ev
        for o in range(2):
            hh = half if o == 0 else 1 - half
            reg = region(block_at(way, d), 1 - c, hh, s)
            remote(reg, reg, c_send.at[way, d - 1, s, o], c_recv.at[way, d - 1, s, o], cdev).wait_recv()

    w_copy.wait()
    lay_out(0, 8)
    lag = 2 * SUBS
    laid = 8
    for k, ev in enumerate(events):
        way, d, s = ev
        reg = region(block_at(way, d), c, half, s)
        remote(reg, reg, z_send.at[way, d - 1, s], z_recv.at[way, d - 1, s], zdev[way]).wait_recv()
        if d < 3 or (d == 3 and s // (SUBS // 2) == way):
            send(reg, reg, z_send.at[way, d, s], z_recv.at[way, d, s], zdev[way])
        send(reg, reg, x_send.at[way, d - 1, s], x_recv.at[way, d - 1, s], xdev[s % 2])
        send(reg, reg, c_send.at[way, d - 1, s, 0], c_recv.at[way, d - 1, s, 0], cdev)
        if k >= lag:
            from_x(events[k - lag])
        upto = 8 + 56 * (k + 1) // len(events)
        if upto > laid:
            lay_out(laid, upto - laid)
            laid = upto
    for ev in events[-lag:]:
        from_x(ev)
    remote(own_rows(1 - c), own_rows(1 - c), own_sem.at[0], own_sem.at[1], cdev).wait_recv()
    for ev in events:
        from_core(ev)

    plan_copy.wait()

    def compact(i, carry):
        xs[pl.ds(pl.multiple_of(i * UNIT, UNIT), UNIT), :] = xg[plans[1, i]]
        return carry

    lax.fori_loop(0, 64, compact, 0)

    turn = (1, 3)

    def dest_of(way, step):
        return lax.rem(yp + 12 - turn[way] * (step + 1), 4)

    def multiply(kind, part):
        for way in range(2):
            rows = slice(way * 512, way * 512 + 512)
            pair = [kind * 4 + dest_of(way, 2 * part + k) for k in range(2)]
            weights = jnp.concatenate([wv[j] for j in pair], axis=1)
            value = jnp.dot(xs[rows, :], weights, preferred_element_type=jnp.float32).astype(jnp.bfloat16)
            yc[pair[0], rows, :] = value[:, :128]
            yc[pair[1], rows, :] = value[:, 128:]

    def rows_of(way, sub):
        return pl.ds(way * 512 + sub * ROWS, ROWS)

    def add(kind, dest, way, sub, step):
        return (
            yc[kind * 4 + dest, rows_of(way, sub), :].astype(jnp.float32)
            + rbuf[way, kind, sub, step].astype(jnp.float32)
        ).astype(jnp.bfloat16)

    def arrived(kind, way, sub, step):
        remote(
            rbuf.at[way, kind, sub, step], rbuf.at[way, kind, sub, step],
            rs_send.at[way, kind, sub, step], rs_recv.at[way, kind, sub, step], ydev[way],
        ).wait_recv()

    def halves(group):
        return range(group * SUBS // 2, (group + 1) * SUBS // 2)

    def hop(kind, step, group):
        for sub in halves(group):
            for way in range(2):
                dest = dest_of(way, step)
                if step == 0:
                    src = yc.at[kind * 4 + dest, rows_of(way, sub), :]
                else:
                    arrived(kind, way, sub, step - 1)
                    sbuf[way, kind, sub, step - 1] = add(kind, dest, way, sub, step - 1)
                    src = sbuf.at[way, kind, sub, step - 1]
                send(
                    src, rbuf.at[way, kind, sub, step],
                    rs_send.at[way, kind, sub, step], rs_recv.at[way, kind, sub, step], ydev[way],
                )

    def kv_rows(section, kind, way, sub):
        units = ROWS // UNIT
        return kv.at[kind - 1, pl.ds(section * 64 + way * 32 + sub * units, units)]

    def final(kind, group):
        for sub in halves(group):
            for way in range(2):
                arrived(kind, way, sub, 2)
                value = add(kind, yp, way, sub, 2)
                if kind == 0:
                    qs[rows_of(way, sub), :] = value
                else:
                    reg = kv_rows(xm, kind, way, sub)
                    reg[...] = value.reshape(ROWS // UNIT, UNIT, 128)
                    for o in range(2):
                        send(
                            reg, reg, g_send.at[o, kind - 1, way, sub],
                            g_recv.at[o, kind - 1, way, sub], xdev[o],
                        )

    def spread(kind, group):
        for sub in halves(group):
            for way in range(2):
                reg = kv_rows(lax.rem(xm + (3, 1)[way], 4), kind, way, sub)
                remote(
                    reg, reg, g_send.at[way, kind - 1, way, sub],
                    g_recv.at[way, kind - 1, way, sub], xdev[way],
                ).wait_recv()
                send(
                    reg, reg, f_send.at[kind - 1, way, sub],
                    f_recv.at[kind - 1, way, sub], xdev[way],
                )

    K, V, Q = 1, 2, 0
    multiply(K, 0)
    hop(K, 0, 0)
    hop(K, 0, 1)
    multiply(V, 0)
    hop(V, 0, 0)
    multiply(K, 1)
    hop(K, 1, 0)
    hop(K, 1, 1)
    hop(V, 0, 1)
    multiply(V, 1)
    hop(K, 2, 0)
    hop(K, 2, 1)
    multiply(Q, 0)
    hop(V, 1, 0)
    hop(V, 1, 1)
    final(K, 0)
    hop(Q, 0, 0)
    final(K, 1)
    multiply(Q, 1)
    hop(V, 2, 0)
    hop(V, 2, 1)
    spread(K, 0)
    hop(Q, 0, 1)
    hop(Q, 1, 0)
    final(V, 0)
    spread(K, 1)
    final(V, 1)
    hop(Q, 1, 1)
    hop(Q, 2, 0)
    hop(Q, 2, 1)
    spread(V, 0)
    spread(V, 1)
    final(Q, 0)
    final(Q, 1)
    for kind in (1, 2):
        for sub in range(SUBS):
            for way in range(2):
                reg = kv_rows(lax.rem(xm + (1, 3)[way], 4), kind, way, sub)
                remote(
                    reg, reg, g_send.at[1 - way, kind - 1, way, sub],
                    g_recv.at[1 - way, kind - 1, way, sub], xdev[1 - way],
                ).wait_recv()
                reg = kv_rows(lax.rem(xm + 2, 4), kind, way, sub)
                remote(
                    reg, reg, f_send.at[kind - 1, way, sub],
                    f_recv.at[kind - 1, way, sub], xdev[way],
                ).wait_recv()

    def order_keys(u, carry):
        to = pl.ds(pl.multiple_of(u * UNIT, UNIT), UNIT)
        unit = plans[0, u]
        kt[to, :] = kv[0, unit]
        vt[to, :] = kv[1, unit]
        return carry

    lax.fori_loop(0, 128, order_keys, 0)

    dests = [lax.rem(z + k, 8) for k in (4, 3, 5, 2, 6, 1, 7, 0)]
    hdev = [ydev[0], opposite, ydev[1]]

    def my_cols(p):
        return pl.ds(pl.multiple_of(p * 128, 128), 128)

    def attend(i):
        d = dests[i]
        query = qs[pl.ds(pl.multiple_of(d * 128, 128), 128), :]
        scores = lax.dot_general(
            query, kt[...], (((1,), (1,)), ((), ())), preferred_element_type=jnp.float32
        ) * (128 ** -0.5)
        base = jnp.concatenate(
            [jnp.full((UNIT, 1), plans[1, d * 8 + k] * UNIT, jnp.int32) for k in range(8)], axis=0
        )
        row = lax.broadcasted_iota(jnp.int32, (128, 1), 0)
        pos = base + lax.rem(row, UNIT)
        key = lax.broadcasted_iota(jnp.int32, (128, 2048), 1)
        scores = jnp.where(key <= pos, scores, NEG)
        top = jnp.max(scores, axis=1, keepdims=True)
        weights = jnp.exp(scores - top)
        total = jnp.sum(weights, axis=1, keepdims=True)
        mixed = jnp.dot(weights.astype(jnp.bfloat16), vt[...], preferred_element_type=jnp.float32)
        heads[i, :, my_cols(yp)] = (mixed / total).astype(jnp.bfloat16)
        mine = heads.at[i, :, my_cols(yp)]
        for k in range(3):
            send(mine, mine, h_send.at[i, k], h_recv.at[i, k], hdev[k])

    def project(i):
        for k in range(3):
            other = heads.at[i, :, my_cols(lax.rem(yp + 3 - k, 4))]
            remote(other, other, h_send.at[i, k], h_recv.at[i, k], hdev[k]).wait_recv()

        def part(j, carry):
            cols = pl.ds(pl.multiple_of(j * 512, 512), 512)
            value = jnp.dot(heads[i], wo[:, cols], preferred_element_type=jnp.float32)
            first = value[:64]
            second = value[64:]
            zown[i, :, cols] = jnp.where(c == 0, first, second)
            csend[i, :, cols] = jnp.where(c == 0, second, first).astype(jnp.bfloat16)
            return carry

        lax.fori_loop(0, 4, part, 0)
        send(csend.at[i], crecv.at[i], p_send.at[i], p_recv.at[i], cdev)

    top_of = {(0, 0): 3, (0, 1): 4, (1, 0): 4, (1, 1): 3}

    def ring(way, dist, part):
        i = {4: 0, 3: 1, 2: 3, 1: 5}[dist] + (1 if way == 1 and dist < 4 else 0)
        cols = slice(part * 1024, part * 1024 + 1024)
        value = zown[i, :, cols] + crecv[i, :, cols].astype(jnp.float32)
        if dist < top_of[(way, part)]:
            came = rrecv.at[way, dist, part]
            remote(
                came, came, r_send.at[way, dist, part], r_recv.at[way, dist, part], zdev[way]
            ).wait_recv()
            value = value + came[...].astype(jnp.float32)
        rsend[way, dist - 1, part] = value.astype(jnp.bfloat16)
        send(
            rsend.at[way, dist - 1, part], rrecv.at[way, dist - 1, part],
            r_send.at[way, dist - 1, part], r_recv.at[way, dist - 1, part], zdev[way],
        )

    def core_sum(i):
        remote(crecv.at[i], crecv.at[i], p_send.at[i], p_recv.at[i], cdev).wait_recv()

    attend(0)
    attend(1)
    wo_copy.wait()
    attend(2)
    project(0)
    attend(3)
    project(1)
    core_sum(0)
    ring(1, 4, 0)
    ring(0, 4, 1)
    attend(4)
    project(2)
    core_sum(1)
    ring(0, 3, 0)
    core_sum(2)
    ring(1, 3, 1)
    attend(5)
    project(3)
    attend(6)
    project(4)
    ring(0, 3, 1)
    ring(1, 3, 0)
    attend(7)
    project(5)
    core_sum(3)
    ring(0, 2, 0)
    core_sum(4)
    ring(1, 2, 1)
    project(6)
    ring(0, 2, 1)
    ring(1, 2, 0)
    project(7)
    core_sum(5)
    ring(0, 1, 0)
    core_sum(6)
    ring(1, 1, 1)
    ring(0, 1, 1)
    ring(1, 1, 0)
    core_sum(7)

    row = lax.broadcasted_iota(jnp.int32, (64, 1), 0) + t * 64
    alive = row < planv[2:3, 0:1] * UNIT
    residual = xs.at[pl.ds(pl.multiple_of(t * 64, 64), 64), :]
    for part in range(2):
        cols = slice(part * 1024, part * 1024 + 1024)
        value = zown[7, :, cols] + crecv[7, :, cols].astype(jnp.float32)
        value = value + residual[:, cols].astype(jnp.float32)
        for way in (part, 1 - part):
            came = rrecv.at[way, 0, part]
            remote(
                came, came, r_send.at[way, 0, part], r_recv.at[way, 0, part], zdev[way]
            ).wait_recv()
            value = value + came[...].astype(jnp.float32)
        out_ref[:, cols] = jnp.where(alive, value, 0.0).astype(jnp.bfloat16)
    for copy in sent:
        copy.wait_send()


def local(hidden_in, spans, w_qkv, w_out):
    bf = jnp.bfloat16
    dma = pltpu.SemaphoreType.DMA
    vmem = pl.BlockSpec(memory_space=pltpu.VMEM)
    anyw = pl.BlockSpec(memory_space=pl.ANY)
    out = pl.pallas_call(
        block_kernel,
        out_shape=jax.ShapeDtypeStruct((64, 2048), bf),
        in_specs=[vmem, anyw, anyw, anyw],
        out_specs=vmem,
        scratch_shapes=[
            pltpu.VMEM((8, 128), jnp.int32),
            pltpu.SMEM((8, 128), jnp.int32),
            pltpu.VMEM((128, UNIT, 2048), bf),
            pltpu.VMEM((24576, 128), bf),
            pltpu.VMEM((384, 128), jnp.float32),
            pltpu.VMEM((12, 2048, 128), bf),
            pltpu.VMEM((512, 2048), bf),
            pltpu.VMEM((1024, 2048), bf),
            pltpu.VMEM((12, 1024, 128), bf),
            pltpu.VMEM((2, 3, SUBS, 2, ROWS, 128), bf),
            pltpu.VMEM((2, 3, SUBS, 3, ROWS, 128), bf),
            pltpu.VMEM((1024, 128), bf),
            pltpu.VMEM((2, 256, UNIT, 128), bf),
            pltpu.VMEM((2048, 128), bf),
            pltpu.VMEM((2048, 128), bf),
            pltpu.VMEM((8, 128, 512), bf),
            pltpu.VMEM((8, 64, 2048), jnp.float32),
            pltpu.VMEM((8, 64, 2048), bf),
            pltpu.VMEM((8, 64, 2048), bf),
            pltpu.VMEM((2, 4, 2, 64, 1024), bf),
            pltpu.VMEM((2, 4, 2, 64, 1024), bf),
            dma((4,)),
            dma((2, 4, SUBS)), dma((2, 4, SUBS)),
            dma((2, 4, SUBS)), dma((2, 4, SUBS)),
            dma((2, 4, SUBS, 2)), dma((2, 4, SUBS, 2)),
            dma((2,)),
            dma((2, 3, SUBS, 3)), dma((2, 3, SUBS, 3)),
            dma((2, 2, 2, SUBS)), dma((2, 2, 2, SUBS)),
            dma((2, 2, SUBS)), dma((2, 2, SUBS)),
            dma((8, 3)), dma((8, 3)),
            dma((8,)), dma((8,)),
            dma((2, 4, 2)), dma((2, 4, 2)),
        ],
        compiler_params=pltpu.CompilerParams(
            collective_id=1, has_side_effects=True, vmem_limit_bytes=60 * 1024 * 1024
        ),
        name="block",
    )(
        spans.T, hidden_in.reshape(8, UNIT, 2048), w_qkv.reshape(24576, 128), w_out.reshape(512, 2048)
    )
    return out[None]


def solution(mesh):
    in_specs = (P("tok", "tp"), P(), P("mod", "tp", None, "tok", None), P("mod", "tok", None, "tp"))
    out_specs = P("mod", "tok", "tp")
    return jax.shard_map(local, mesh=mesh, in_specs=in_specs, out_specs=out_specs, check_vma=False)
```

```python
import jax
import jax.numpy as jnp
from jax import lax
from jax.experimental import pallas as pl
from jax.experimental.pallas import tpu as pltpu
from jax.sharding import PartitionSpec as P

MESH = pl.DeviceIdType.MESH
UNIT = 16
NEG = -1e30


def remote(src, dst, send, recv, dev):
    return pltpu.make_async_remote_copy(
        src_ref=src, dst_ref=dst, send_sem=send, recv_sem=recv, device_id=dev, device_id_type=MESH
    )


def greet(devs):
    barrier = pltpu.get_barrier_semaphore()
    for dev in devs:
        pl.semaphore_signal(barrier, inc=1, device_id=dev, device_id_type=MESH)
    pl.semaphore_wait(barrier, len(devs))


def where_am_i():
    t = lax.axis_index("tok")
    return lax.axis_index("mod"), lax.div(t, 2), lax.rem(t, 2), lax.axis_index("tp")


STAGGER = 10
SUBS = 4
PIECE = 1024 // SUBS
GROUPS = 2
ROWS = 512 // GROUPS


def make_plan(spans_ref, planv, me):
    down = lax.broadcasted_iota(jnp.int32, (128, 128), 0)
    across = lax.broadcasted_iota(jnp.int32, (128, 128), 1)
    eye = down == across

    def column(row):
        return jnp.sum(jnp.where(eye, row, 0), axis=1, keepdims=True)

    start = spans_ref[0:1, :]
    first = column(start)
    end = column(start + spans_ref[1:2, :])
    kind = column(spans_ref[2:3, :])
    at = across * UNIT
    inside = (at >= first) & (at < end)
    unit_mod = jnp.sum(jnp.where(inside, kind, 0), axis=0, keepdims=True)
    mod_col = column(unit_mod)
    before = (mod_col == unit_mod) & (down < across)
    rank = jnp.sum(jnp.where(before, 1, 0), axis=0, keepdims=True)
    mine = (mod_col == me) & (column(rank) == across)
    planv[0:1, :] = unit_mod * 64 + rank
    planv[1:2, :] = jnp.sum(jnp.where(mine, down, 0), axis=0, keepdims=True)
    live = jnp.sum(jnp.where(unit_mod == me, 1, 0), axis=1, keepdims=True)
    planv[2:3, :] = jnp.broadcast_to(live, (1, 128))


def block_kernel(
    spans_ref, hid_ref, w_ref, wo_ref,
    out_ref,
    planv, plans, xg, wr, wf, wv, wo, xs, yc, sbuf, rbuf, qs, keys, values,
    kt, vt, probs, totals, heads, zown, csend, crecv, rsend, rrecv,
    local_sem, w_sem, sent_sem, z_recv, x_recv, c_recv, rs_recv, g_recv, gf_recv,
    h_recv, p_recv, r_recv,
):
    xm, z, c, yp = where_am_i()
    t = z * 2 + c
    half = lax.rem(xm, 2)
    zdev = [{"tok": lax.rem(z + 1, 8) * 2 + c}, {"tok": lax.rem(z + 7, 8) * 2 + c}]
    xdev = [{"mod": lax.rem(xm + 1, 4)}, {"mod": lax.rem(xm + 3, 4)}]
    ydev = [{"tp": lax.rem(yp + 1, 4)}, {"tp": lax.rem(yp + 3, 4)}]
    opposite = {"tp": lax.rem(yp + 2, 4)}
    cdev = {"tok": z * 2 + 1 - c}

    def region(zz, cc, hh, s):
        return xg.at[hh * SUBS + s, pl.ds((zz * 2 + cc) * 8, 8)]

    def own_rows(cc):
        return xg.at[:, pl.ds((z * 2 + cc) * 8, 8)]

    def block_at(way, d):
        return lax.rem(z + 8 - d, 8) if way == 0 else lax.rem(z + d, 8)

    hid_copies = [
        pltpu.make_async_copy(
            hid_ref.at[:, :, p * PIECE:(p + 1) * PIECE],
            xg.at[p, pl.ds((z * 2 + c) * 8, 8)],
            local_sem.at[0],
        )
        for p in range(2 * SUBS)
    ]
    for copy in hid_copies:
        copy.start()
    w_copies = []
    for k in range(4):
        part = pl.ds(k * 6144, 6144)
        w_copies.append(pltpu.make_async_copy(w_ref.at[part], wr.at[part], w_sem.at[k]))
        w_copies[k].start()
    wo_copy = pltpu.make_async_copy(wo_ref, wo, local_sem.at[2])
    wo_copy.start()
    greet(zdev + xdev + ydev + [opposite, cdev])
    pltpu.make_async_copy(own_rows(c), own_rows(c), local_sem.at[0]).wait()

    def send(src, dst, line, rsem, dev):
        remote(src, dst, sent_sem.at[line], rsem, dev).start()

    def arrive(ref, rsem):
        remote(ref, ref, sent_sem.at[0], rsem, cdev).wait_recv()

    def left(ref, line):
        remote(ref, ref, sent_sem.at[line], c_recv.at[0], cdev).wait_send()

    events = []
    for d in range(1, 5):
        for s in range(SUBS):
            for way in range(2):
                if d < 4 or s // (SUBS // 2) == way:
                    events.append((way, d, s))
    events[-SUBS:] = [(s // (SUBS // 2), 4, s) for k in range(SUBS // 2) for s in (k, k + SUBS // 2)]
    event_at = {ev: k for k, ev in enumerate(events)}

    def lay_out(first, count):
        def step(i, carry):
            at = pl.multiple_of((first + i) * 32, 32)
            wf[...] = wr[pl.ds(pl.multiple_of(at * 12, 384), 384), :].astype(jnp.float32)
            for j in range(12):
                rows = wf[pl.ds(j, 32, stride=12), :]
                wv[j, pl.ds(at, 32), :] = rows.astype(jnp.bfloat16)
            return carry

        lax.fori_loop(0, count, step, 0)

    laid = 0
    for s in range(SUBS):
        for way in range(2):
            reg = region(z, c, half, s)
            send(reg, reg, 0, z_recv.at[event_at[way, 1, s]], zdev[way])
        if s == 0:
            make_plan(spans_ref, planv, xm)
            plan_copy = pltpu.make_async_copy(planv, plans, local_sem.at[3])
            plan_copy.start()
        elif s < SUBS - 1:
            w_copies[s - 1].wait()
            lay_out(laid, STAGGER)
            laid += STAGGER
    send(own_rows(c), own_rows(c), 2, c_recv.at[0], cdev)
    for copy in w_copies[2:]:
        copy.wait()

    def from_x(k):
        way, d, s = events[k]
        reg = region(block_at(way, d), c, 1 - half, s)
        arrive(reg, x_recv.at[k])
        send(reg, reg, 2, c_recv.at[0], cdev)

    lag = 2 * SUBS
    for k, ev in enumerate(events):
        way, d, s = ev
        reg = region(block_at(way, d), c, half, s)
        arrive(reg, z_recv.at[k])
        if d < 3 or (d == 3 and s // (SUBS // 2) == way):
            send(reg, reg, 0, z_recv.at[event_at[way, d + 1, s]], zdev[way])
        send(reg, reg, 1, x_recv.at[k], xdev[s % 2])
        send(reg, reg, 2, c_recv.at[0], cdev)
        if k >= lag:
            from_x(k - lag)
        upto = 2 * STAGGER + (64 - 2 * STAGGER) * (k + 1) // len(events)
        if upto > laid:
            lay_out(laid, upto - laid)
            laid = upto
    for k in range(len(events) - lag, len(events)):
        from_x(k)
    arrive(xg.at[:, 0:64], c_recv.at[0])

    plan_copy.wait()

    def compact(i, carry):
        unit = plans[1, i]
        to = pl.ds(pl.multiple_of(i * UNIT, UNIT), UNIT)
        for p in range(2 * SUBS):
            xs[to, p * PIECE:(p + 1) * PIECE] = xg[p, unit]
        return carry

    lax.fori_loop(0, 64, compact, 0)

    turn = (1, 3)

    def dest_of(way, step):
        return lax.rem(yp + 12 - turn[way] * (step + 1), 4)

    def multiply(kind, part):
        for way in range(2):
            rows = slice(way * 512, way * 512 + 512)
            pair = [kind * 4 + dest_of(way, 2 * part + k) for k in range(2)]
            weights = jnp.concatenate([wv[j] for j in pair], axis=1)
            value = jnp.dot(xs[rows, :], weights, preferred_element_type=jnp.float32).astype(jnp.bfloat16)
            yc[pair[0], rows, :] = value[:, :128]
            yc[pair[1], rows, :] = value[:, 128:]

    def rows_of(way, sub):
        return pl.ds(way * 512 + sub * ROWS, ROWS)

    def add(kind, dest, way, sub, step):
        return (
            yc[kind * 4 + dest, rows_of(way, sub), :].astype(jnp.float32)
            + rbuf[way, kind, sub, step].astype(jnp.float32)
        ).astype(jnp.bfloat16)

    def arrived(kind, way, sub, step):
        arrive(rbuf.at[way, kind, sub, step], rs_recv.at[way, kind, sub, step])

    def hop(kind, step, sub):
        for way in range(2):
            dest = dest_of(way, step)
            if step == 0:
                src = yc.at[kind * 4 + dest, rows_of(way, sub), :]
            else:
                arrived(kind, way, sub, step - 1)
                sbuf[way, kind, sub, step - 1] = add(kind, dest, way, sub, step - 1)
                src = sbuf.at[way, kind, sub, step - 1]
            send(src, rbuf.at[way, kind, sub, step], 3, rs_recv.at[way, kind, sub, step], ydev[way])

    kv = (keys, values)

    def kv_rows(section, kind, way, sub):
        units = ROWS // UNIT
        return kv[kind - 1].at[pl.ds(section * 64 + way * 32 + sub * units, units)]

    def final(kind, sub):
        for way in range(2):
            arrived(kind, way, sub, 2)
            value = add(kind, yp, way, sub, 2)
            if kind == 0:
                qs[rows_of(way, sub), :] = value
            else:
                reg = kv_rows(xm, kind, way, sub)
                reg[...] = value.reshape(ROWS // UNIT, UNIT, 128)
                send(reg, reg, 4, g_recv.at[kind - 1, way, sub], xdev[way])
                send(reg, reg, 4, gf_recv.at[kind - 1], xdev[1 - way])

    def spread(kind, sub):
        for way in range(2):
            reg = kv_rows(lax.rem(xm + (3, 1)[way], 4), kind, way, sub)
            arrive(reg, g_recv.at[kind - 1, way, sub])
            send(reg, reg, 5, gf_recv.at[kind - 1], xdev[way])

    K, V, Q = 1, 2, 0
    multiply(K, 0)
    hop(K, 0, 0)
    hop(K, 0, 1)
    multiply(V, 0)
    hop(V, 0, 0)
    multiply(K, 1)
    hop(K, 1, 0)
    hop(K, 1, 1)
    hop(V, 0, 1)
    multiply(V, 1)
    hop(K, 2, 0)
    hop(K, 2, 1)
    multiply(Q, 0)
    hop(V, 1, 0)
    hop(V, 1, 1)
    final(K, 0)
    hop(Q, 0, 0)
    final(K, 1)
    multiply(Q, 1)
    hop(V, 2, 0)
    hop(V, 2, 1)
    spread(K, 0)
    hop(Q, 0, 1)
    hop(Q, 1, 0)
    final(V, 0)
    spread(K, 1)
    final(V, 1)
    hop(Q, 1, 1)
    hop(Q, 2, 0)
    hop(Q, 2, 1)
    spread(V, 0)
    spread(V, 1)

    def in_token_order(kind, to_ref):
        arrive(kv[kind - 1].at[0:128], gf_recv.at[kind - 1])

        def step(i, carry):
            for k in range(4):
                u = i * 4 + k
                to_ref[pl.ds(pl.multiple_of(u * UNIT, UNIT), UNIT), :] = kv[kind - 1][plans[0, u]]
            return carry

        lax.fori_loop(0, 32, step, 0)

    in_token_order(K, kt)
    final(Q, 0)
    final(Q, 1)

    dests = [lax.rem(z + k, 8) for k in (4, 3, 5, 2, 6, 1, 7, 0)]
    hdev = [ydev[0], opposite, ydev[1]]

    def my_cols(p):
        return pl.ds(pl.multiple_of(p * 128, 128), 128)

    def score(i):
        d = dests[i]
        query = qs[pl.ds(pl.multiple_of(d * 128, 128), 128), :]
        scores = lax.dot_general(
            query, kt[...], (((1,), (1,)), ((), ())), preferred_element_type=jnp.float32
        ) * (128 ** -0.5)
        base = jnp.concatenate(
            [jnp.full((UNIT, 1), plans[1, d * 8 + k] * UNIT, jnp.int32) for k in range(8)], axis=0
        )
        row = lax.broadcasted_iota(jnp.int32, (128, 1), 0)
        pos = base + lax.rem(row, UNIT)
        key = lax.broadcasted_iota(jnp.int32, (128, 2048), 1)
        scores = jnp.where(key <= pos, scores, NEG)
        top = jnp.max(scores, axis=1, keepdims=True)
        weights = jnp.exp(scores - top)
        totals[i] = jnp.sum(weights, axis=1, keepdims=True)
        probs[i] = weights.astype(jnp.bfloat16)

    def mix(i):
        mixed = jnp.dot(probs[i], vt[...], preferred_element_type=jnp.float32)
        heads[i, :, my_cols(yp)] = (mixed / totals[i]).astype(jnp.bfloat16)
        mine = heads.at[i, :, my_cols(yp)]
        for k in range(3):
            send(mine, mine, 6, h_recv.at[i], hdev[k])

    def project(i):
        arrive(heads.at[i, :, 0:384], h_recv.at[i])

        def part(j, carry):
            cols = pl.ds(pl.multiple_of(j * 512, 512), 512)
            value = jnp.dot(heads[i], wo[:, cols], preferred_element_type=jnp.float32)
            first = value[:64]
            second = value[64:]
            zown[i, :, cols] = jnp.where(c == 0, first, second)
            csend[i, :, cols] = jnp.where(c == 0, second, first).astype(jnp.bfloat16)
            return carry

        lax.fori_loop(0, 4, part, 0)
        send(csend.at[i], crecv.at[i], 7, p_recv.at[i], cdev)

    top_of = {(0, 0): 3, (0, 1): 4, (1, 0): 4, (1, 1): 3}

    def number(way, dist, part, q):
        if dist < 4:
            return (((way * 3 + dist - 1) * 2) + part) * 2 + q
        return 24 + way * 2 + q

    def ring(way, dist, part):
        i = {4: 0, 3: 1, 2: 3, 1: 5}[dist] + (1 if way == 1 and dist < 4 else 0)
        for q in range(2):
            cols = slice(part * 1024 + q * 512, part * 1024 + q * 512 + 512)
            value = zown[i, :, cols] + crecv[i, :, cols].astype(jnp.float32)
            if dist < top_of[(way, part)]:
                came = number(way, dist + 1, part, q)
                arrive(rrecv.at[came], r_recv.at[came])
                value = value + rrecv[came].astype(jnp.float32)
            n = number(way, dist, part, q)
            rsend[n] = value.astype(jnp.bfloat16)
            send(rsend.at[n], rrecv.at[n], 8, r_recv.at[n], zdev[way])

    def core_sum(i):
        arrive(crecv.at[i], p_recv.at[i])

    def both(*ops):
        for op in ops:
            ring(*op)

    score(0)
    score(1)
    score(2)
    wo_copy.wait()
    in_token_order(V, vt)
    mix(0)
    mix(1)
    mix(2)
    score(3)
    project(0)
    mix(3)
    project(1)
    core_sum(0)
    both((1, 4, 0), (0, 4, 1))
    project(2)
    score(4)
    mix(4)
    core_sum(1)
    core_sum(2)
    both((0, 3, 0), (1, 3, 1))
    project(3)
    score(5)
    mix(5)
    project(4)
    score(6)
    mix(6)
    both((0, 3, 1), (1, 3, 0))
    project(5)
    score(7)
    mix(7)
    core_sum(3)
    core_sum(4)
    both((0, 2, 0), (1, 2, 1))
    project(6)
    both((0, 2, 1), (1, 2, 0))
    project(7)
    core_sum(5)
    core_sum(6)
    both((0, 1, 0), (1, 1, 1), (0, 1, 1), (1, 1, 0))
    core_sum(7)

    row = lax.broadcasted_iota(jnp.int32, (64, 1), 0) + t * 64
    alive = row < planv[2:3, 0:1] * UNIT
    residual = xs.at[pl.ds(pl.multiple_of(t * 64, 64), 64), :]
    for part in range(2):
        for q in range(2):
            cols = slice(part * 1024 + q * 512, part * 1024 + q * 512 + 512)
            value = zown[7, :, cols] + crecv[7, :, cols].astype(jnp.float32)
            value = value + residual[:, cols].astype(jnp.float32)
            for way in (part, 1 - part):
                came = number(way, 1, part, q)
                arrive(rrecv.at[came], r_recv.at[came])
                value = value + rrecv[came].astype(jnp.float32)
            out_ref[:, cols] = jnp.where(alive, value, 0.0).astype(jnp.bfloat16)
    left(xg.at[0:7, 0:32], 0)
    left(xg.at[0:7, 0:32], 1)
    left(xg.at[:, 0:64], 2)
    left(rbuf, 3)
    left(keys, 4)
    left(keys.at[0:128], 5)
    left(heads.at[:, :, 0:384], 6)
    left(csend, 7)
    left(rsend, 8)


def local(hidden_in, spans, w_qkv, w_out):
    bf = jnp.bfloat16
    dma = pltpu.SemaphoreType.DMA
    vmem = pl.BlockSpec(memory_space=pltpu.VMEM)
    anyw = pl.BlockSpec(memory_space=pl.ANY)
    out = pl.pallas_call(
        block_kernel,
        out_shape=jax.ShapeDtypeStruct((64, 2048), bf),
        in_specs=[vmem, anyw, anyw, anyw],
        out_specs=vmem,
        scratch_shapes=[
            pltpu.VMEM((8, 128), jnp.int32),
            pltpu.SMEM((8, 128), jnp.int32),
            pltpu.VMEM((2 * SUBS, 128, UNIT, PIECE), bf),
            pltpu.VMEM((24576, 128), bf),
            pltpu.VMEM((384, 128), jnp.float32),
            pltpu.VMEM((12, 2048, 128), bf),
            pltpu.VMEM((512, 2048), bf),
            pltpu.VMEM((1024, 2048), bf),
            pltpu.VMEM((12, 1024, 128), bf),
            pltpu.VMEM((2, 3, GROUPS, 2, ROWS, 128), bf),
            pltpu.VMEM((2, 3, GROUPS, 3, ROWS, 128), bf),
            pltpu.VMEM((1024, 128), bf),
            pltpu.VMEM((256, UNIT, 128), bf),
            pltpu.VMEM((256, UNIT, 128), bf),
            pltpu.VMEM((2048, 128), bf),
            pltpu.VMEM((2048, 128), bf),
            pltpu.VMEM((8, 128, 2048), bf),
            pltpu.VMEM((8, 128, 1), jnp.float32),
            pltpu.VMEM((8, 128, 512), bf),
            pltpu.VMEM((8, 64, 2048), jnp.float32),
            pltpu.VMEM((8, 64, 2048), bf),
            pltpu.VMEM((8, 64, 2048), bf),
            pltpu.VMEM((28, 64, 512), bf),
            pltpu.VMEM((28, 64, 512), bf),
            dma((4,)), dma((4,)), dma((9,)),
            dma((28,)), dma((28,)), dma((1,)),
            dma((2, 3, GROUPS, 3)), dma((2, 2, GROUPS)), dma((2,)),
            dma((8,)), dma((8,)), dma((28,)),
        ],
        compiler_params=pltpu.CompilerParams(
            collective_id=1, has_side_effects=True, vmem_limit_bytes=60 * 1024 * 1024
        ),
        name="block",
    )(
        spans.T, hidden_in.reshape(8, UNIT, 2048), w_qkv.reshape(24576, 128), w_out.reshape(512, 2048)
    )
    return out[None]


def solution(mesh):
    in_specs = (P("tok", "tp"), P(), P("mod", "tp", None, "tok", None), P("mod", "tok", None, "tp"))
    out_specs = P("mod", "tok", "tp")
    return jax.shard_map(local, mesh=mesh, in_specs=in_specs, out_specs=out_specs, check_vma=False)
```

```python
import jax
import jax.numpy as jnp
from jax import lax
from jax.experimental import pallas as pl
from jax.experimental.pallas import tpu as pltpu
from jax.sharding import PartitionSpec as P

MESH = pl.DeviceIdType.MESH
UNIT = 16
NEG = -1e30


def remote(src, dst, send, recv, dev):
    return pltpu.make_async_remote_copy(
        src_ref=src, dst_ref=dst, send_sem=send, recv_sem=recv, device_id=dev, device_id_type=MESH
    )


def greet(devs):
    barrier = pltpu.get_barrier_semaphore()
    for dev in devs:
        pl.semaphore_signal(barrier, inc=1, device_id=dev, device_id_type=MESH)
    pl.semaphore_wait(barrier, len(devs))


def where_am_i():
    t = lax.axis_index("tok")
    return lax.axis_index("mod"), lax.div(t, 2), lax.rem(t, 2), lax.axis_index("tp")


STAGGER = 10
SUBS = 4
PIECE = 1024 // SUBS
GROUPS = 2
ROWS = 512 // GROUPS


def make_plan(spans_ref, planv, me):
    down = lax.broadcasted_iota(jnp.int32, (128, 128), 0)
    across = lax.broadcasted_iota(jnp.int32, (128, 128), 1)
    eye = down == across

    def column(row):
        return jnp.sum(jnp.where(eye, row, 0), axis=1, keepdims=True)

    start = spans_ref[0:1, :]
    first = column(start)
    end = column(start + spans_ref[1:2, :])
    kind = column(spans_ref[2:3, :])
    at = across * UNIT
    inside = (at >= first) & (at < end)
    unit_mod = jnp.sum(jnp.where(inside, kind, 0), axis=0, keepdims=True)
    mod_col = column(unit_mod)
    before = (mod_col == unit_mod) & (down < across)
    rank = jnp.sum(jnp.where(before, 1, 0), axis=0, keepdims=True)
    mine = (mod_col == me) & (column(rank) == across)
    planv[0:1, :] = unit_mod * 64 + rank
    planv[1:2, :] = jnp.sum(jnp.where(mine, down, 0), axis=0, keepdims=True)
    live = jnp.sum(jnp.where(unit_mod == me, 1, 0), axis=1, keepdims=True)
    planv[2:3, :] = jnp.broadcast_to(live, (1, 128))


def block_kernel(
    spans_ref, hid_ref, w_ref, wo_ref,
    out_ref,
    planv, plans, xg, wr, wf, wv, wo, xs, yc, sbuf, rbuf, qs, keys, values,
    kt, vt, probs, totals, heads, zown, csend, crecv, rsend, rrecv,
    local_sem, w_sem, sent_sem, z_recv, x_recv, c_recv, rs_recv, g_recv, gf_recv,
    h_recv, p_recv, r_recv,
):
    xm, z, c, yp = where_am_i()
    t = z * 2 + c
    half = lax.rem(xm, 2)
    zdev = [{"tok": lax.rem(z + 1, 8) * 2 + c}, {"tok": lax.rem(z + 7, 8) * 2 + c}]
    xdev = [{"mod": lax.rem(xm + 1, 4)}, {"mod": lax.rem(xm + 3, 4)}]
    ydev = [{"tp": lax.rem(yp + 1, 4)}, {"tp": lax.rem(yp + 3, 4)}]
    opposite = {"tp": lax.rem(yp + 2, 4)}
    cdev = {"tok": z * 2 + 1 - c}

    def region(zz, cc, hh, s):
        return xg.at[hh * SUBS + s, pl.ds((zz * 2 + cc) * 8, 8)]

    def own_rows(cc):
        return xg.at[:, pl.ds((z * 2 + cc) * 8, 8)]

    def block_at(way, d):
        return lax.rem(z + 8 - d, 8) if way == 0 else lax.rem(z + d, 8)

    hid_copies = [
        pltpu.make_async_copy(
            hid_ref.at[:, :, p * PIECE:(p + 1) * PIECE],
            xg.at[p, pl.ds((z * 2 + c) * 8, 8)],
            local_sem.at[0],
        )
        for p in range(2 * SUBS)
    ]
    for copy in hid_copies:
        copy.start()
    w_copies = []
    for k in range(4):
        part = pl.ds(k * 6144, 6144)
        w_copies.append(pltpu.make_async_copy(w_ref.at[part], wr.at[part], w_sem.at[k]))
        w_copies[k].start()
    wo_copy = pltpu.make_async_copy(wo_ref, wo, local_sem.at[2])
    wo_copy.start()
    greet(zdev + xdev + ydev + [opposite, cdev])
    pltpu.make_async_copy(own_rows(c), own_rows(c), local_sem.at[0]).wait()

    def send(src, dst, line, rsem, dev):
        remote(src, dst, sent_sem.at[line], rsem, dev).start()

    def arrive(ref, rsem):
        remote(ref, ref, sent_sem.at[0], rsem, cdev).wait_recv()

    def left(ref, line):
        remote(ref, ref, sent_sem.at[line], c_recv.at[0], cdev).wait_send()

    events = []
    for d in range(1, 5):
        for s in range(SUBS):
            for way in range(2):
                if d < 4 or s // (SUBS // 2) == way:
                    events.append((way, d, s))
    events[-SUBS:] = [(s // (SUBS // 2), 4, s) for k in range(SUBS // 2) for s in (k, k + SUBS // 2)]
    event_at = {ev: k for k, ev in enumerate(events)}

    def lay_out(first, count):
        def step(i, carry):
            at = pl.multiple_of((first + i) * 32, 32)
            wf[...] = wr[pl.ds(pl.multiple_of(at * 12, 384), 384), :].astype(jnp.float32)
            for j in range(12):
                rows = wf[pl.ds(j, 32, stride=12), :]
                wv[j, pl.ds(at, 32), :] = rows.astype(jnp.bfloat16)
            return carry

        lax.fori_loop(0, count, step, 0)

    laid = 0
    for s in range(SUBS):
        for way in range(2):
            reg = region(z, c, half, s)
            send(reg, reg, 0, z_recv.at[event_at[way, 1, s]], zdev[way])
        if s == 0:
            make_plan(spans_ref, planv, xm)
            plan_copy = pltpu.make_async_copy(planv, plans, local_sem.at[3])
            plan_copy.start()
        elif s < SUBS - 1:
            w_copies[s - 1].wait()
            lay_out(laid, STAGGER)
            laid += STAGGER
    send(own_rows(c), own_rows(c), 2, c_recv.at[0], cdev)
    for copy in w_copies[2:]:
        copy.wait()

    def from_x(k):
        way, d, s = events[k]
        reg = region(block_at(way, d), c, 1 - half, s)
        arrive(reg, x_recv.at[k])
        send(reg, reg, 2, c_recv.at[0], cdev)

    lag = 2 * SUBS
    for k, ev in enumerate(events):
        way, d, s = ev
        reg = region(block_at(way, d), c, half, s)
        arrive(reg, z_recv.at[k])
        if d < 3 or (d == 3 and s // (SUBS // 2) == way):
            send(reg, reg, 0, z_recv.at[event_at[way, d + 1, s]], zdev[way])
        send(reg, reg, 1, x_recv.at[k], xdev[s % 2])
        send(reg, reg, 2, c_recv.at[0], cdev)
        if k >= lag:
            from_x(k - lag)
        upto = 2 * STAGGER + (64 - 2 * STAGGER) * (k + 1) // len(events)
        if upto > laid:
            lay_out(laid, upto - laid)
            laid = upto
    for k in range(len(events) - lag, len(events)):
        from_x(k)
    arrive(xg.at[:, 0:64], c_recv.at[0])

    plan_copy.wait()

    def compact(i, carry):
        for k in range(4):
            unit = plans[1, i * 4 + k]
            to = pl.ds(pl.multiple_of((i * 4 + k) * UNIT, UNIT), UNIT)
            for p in range(2 * SUBS):
                xs[to, p * PIECE:(p + 1) * PIECE] = xg[p, unit]
        return carry

    lax.fori_loop(0, 16, compact, 0)

    turn = (1, 3)

    def dest_of(way, step):
        return lax.rem(yp + 12 - turn[way] * (step + 1), 4)

    def multiply(kind, part, first=0, count=512):
        for way in range(2):
            rows = slice(way * 512 + first, way * 512 + first + count)
            pair = [kind * 4 + dest_of(way, 2 * part + k) for k in range(2)]
            weights = jnp.concatenate([wv[j] for j in pair], axis=1)
            value = jnp.dot(xs[rows, :], weights, preferred_element_type=jnp.float32).astype(jnp.bfloat16)
            yc[pair[0], rows, :] = value[:, :128]
            yc[pair[1], rows, :] = value[:, 128:]

    def rows_of(way, sub):
        return pl.ds(way * 512 + sub * ROWS, ROWS)

    def add(kind, dest, way, sub, step):
        return (
            yc[kind * 4 + dest, rows_of(way, sub), :].astype(jnp.float32)
            + rbuf[way, kind, sub, step].astype(jnp.float32)
        ).astype(jnp.bfloat16)

    def arrived(kind, way, sub, step):
        arrive(rbuf.at[way, kind, sub, step], rs_recv.at[way, kind, sub, step])

    def hop(kind, step, sub):
        for way in range(2):
            dest = dest_of(way, step)
            if step == 0:
                src = yc.at[kind * 4 + dest, rows_of(way, sub), :]
            else:
                arrived(kind, way, sub, step - 1)
                sbuf[way, kind, sub, step - 1] = add(kind, dest, way, sub, step - 1)
                src = sbuf.at[way, kind, sub, step - 1]
            send(src, rbuf.at[way, kind, sub, step], 3, rs_recv.at[way, kind, sub, step], ydev[way])

    kv = (keys, values)

    def kv_rows(section, kind, way, sub):
        units = ROWS // UNIT
        return kv[kind - 1].at[pl.ds(section * 64 + way * 32 + sub * units, units)]

    def final(kind, sub):
        for way in range(2):
            arrived(kind, way, sub, 2)
            value = add(kind, yp, way, sub, 2)
            if kind == 0:
                qs[rows_of(way, sub), :] = value
            else:
                reg = kv_rows(xm, kind, way, sub)
                reg[...] = value.reshape(ROWS // UNIT, UNIT, 128)
                send(reg, reg, 4, g_recv.at[kind - 1, way, sub], xdev[way])
                send(reg, reg, 4, gf_recv.at[kind - 1], xdev[1 - way])

    def spread(kind, sub):
        for way in range(2):
            reg = kv_rows(lax.rem(xm + (3, 1)[way], 4), kind, way, sub)
            arrive(reg, g_recv.at[kind - 1, way, sub])
            send(reg, reg, 5, gf_recv.at[kind - 1], xdev[way])

    K, V, Q = 1, 2, 0
    multiply(K, 0, 0, ROWS)
    hop(K, 0, 0)
    multiply(K, 0, ROWS, ROWS)
    hop(K, 0, 1)
    multiply(V, 0)
    hop(V, 0, 0)
    multiply(K, 1)
    hop(K, 1, 0)
    hop(K, 1, 1)
    hop(V, 0, 1)
    multiply(V, 1)
    hop(K, 2, 0)
    hop(K, 2, 1)
    multiply(Q, 0)
    hop(V, 1, 0)
    hop(V, 1, 1)
    final(K, 0)
    hop(Q, 0, 0)
    final(K, 1)
    multiply(Q, 1)
    hop(V, 2, 0)
    hop(V, 2, 1)
    spread(K, 0)
    hop(Q, 0, 1)
    hop(Q, 1, 0)
    final(V, 0)
    spread(K, 1)
    final(V, 1)
    hop(Q, 1, 1)
    hop(Q, 2, 0)
    hop(Q, 2, 1)
    spread(V, 0)
    spread(V, 1)

    def in_token_order(kind, to_ref):
        arrive(kv[kind - 1].at[0:128], gf_recv.at[kind - 1])

        def step(i, carry):
            for k in range(4):
                u = i * 4 + k
                to_ref[pl.ds(pl.multiple_of(u * UNIT, UNIT), UNIT), :] = kv[kind - 1][plans[0, u]]
            return carry

        lax.fori_loop(0, 32, step, 0)

    in_token_order(K, kt)
    final(Q, 0)
    final(Q, 1)

    dests = [lax.rem(z + k, 8) for k in (4, 3, 5, 2, 6, 1, 7, 0)]
    hdev = [ydev[0], opposite, ydev[1]]

    def my_cols(p):
        return pl.ds(pl.multiple_of(p * 128, 128), 128)

    def score(i):
        d = dests[i]
        query = qs[pl.ds(pl.multiple_of(d * 128, 128), 128), :]
        scores = lax.dot_general(
            query, kt[...], (((1,), (1,)), ((), ())), preferred_element_type=jnp.float32
        ) * (128 ** -0.5)
        base = jnp.concatenate(
            [jnp.full((UNIT, 1), plans[1, d * 8 + k] * UNIT, jnp.int32) for k in range(8)], axis=0
        )
        row = lax.broadcasted_iota(jnp.int32, (128, 1), 0)
        pos = base + lax.rem(row, UNIT)
        key = lax.broadcasted_iota(jnp.int32, (128, 2048), 1)
        scores = jnp.where(key <= pos, scores, NEG)
        top = jnp.max(scores, axis=1, keepdims=True)
        weights = jnp.exp(scores - top)
        totals[i] = jnp.sum(weights, axis=1, keepdims=True)
        probs[i] = weights.astype(jnp.bfloat16)

    def mix(i):
        mixed = jnp.dot(probs[i], vt[...], preferred_element_type=jnp.float32)
        heads[i, :, my_cols(yp)] = (mixed / totals[i]).astype(jnp.bfloat16)
        mine = heads.at[i, :, my_cols(yp)]
        for k in range(3):
            send(mine, mine, 6, h_recv.at[i], hdev[k])

    def project(i):
        arrive(heads.at[i, :, 0:384], h_recv.at[i])

        def part(j, carry):
            cols = pl.ds(pl.multiple_of(j * 512, 512), 512)
            value = jnp.dot(heads[i], wo[:, cols], preferred_element_type=jnp.float32)
            first = value[:64]
            second = value[64:]
            zown[i, :, cols] = jnp.where(c == 0, first, second)
            csend[i, :, cols] = jnp.where(c == 0, second, first).astype(jnp.bfloat16)
            return carry

        lax.fori_loop(0, 4, part, 0)
        send(csend.at[i], crecv.at[i], 7, p_recv.at[i], cdev)

    top_of = {(0, 0): 3, (0, 1): 4, (1, 0): 4, (1, 1): 3}

    def number(way, dist, part, q):
        if dist < 4:
            return (((way * 3 + dist - 1) * 2) + part) * 2 + q
        return 24 + way * 2 + q

    def ring(way, dist, part):
        i = {4: 0, 3: 1, 2: 3, 1: 5}[dist] + (1 if way == 1 and dist < 4 else 0)
        for q in range(2):
            cols = slice(part * 1024 + q * 512, part * 1024 + q * 512 + 512)
            value = zown[i, :, cols] + crecv[i, :, cols].astype(jnp.float32)
            if dist < top_of[(way, part)]:
                came = number(way, dist + 1, part, q)
                arrive(rrecv.at[came], r_recv.at[came])
                value = value + rrecv[came].astype(jnp.float32)
            n = number(way, dist, part, q)
            rsend[n] = value.astype(jnp.bfloat16)
            send(rsend.at[n], rrecv.at[n], 8, r_recv.at[n], zdev[way])

    def core_sum(i):
        arrive(crecv.at[i], p_recv.at[i])

    def both(*ops):
        for op in ops:
            ring(*op)

    score(0)
    score(1)
    score(2)
    wo_copy.wait()
    in_token_order(V, vt)
    mix(0)
    mix(1)
    mix(2)
    score(3)
    project(0)
    mix(3)
    project(1)
    core_sum(0)
    both((1, 4, 0), (0, 4, 1))
    project(2)
    score(4)
    mix(4)
    core_sum(1)
    core_sum(2)
    both((0, 3, 0), (1, 3, 1))
    project(3)
    score(5)
    mix(5)
    project(4)
    score(6)
    mix(6)
    both((0, 3, 1), (1, 3, 0))
    project(5)
    score(7)
    mix(7)
    core_sum(3)
    core_sum(4)
    both((0, 2, 0), (1, 2, 1))
    project(6)
    both((0, 2, 1), (1, 2, 0))
    project(7)
    core_sum(5)
    core_sum(6)
    both((0, 1, 0), (1, 1, 1), (0, 1, 1), (1, 1, 0))
    core_sum(7)

    row = lax.broadcasted_iota(jnp.int32, (64, 1), 0) + t * 64
    alive = row < planv[2:3, 0:1] * UNIT
    residual = xs.at[pl.ds(pl.multiple_of(t * 64, 64), 64), :]
    for part in range(2):
        for q in range(2):
            cols = slice(part * 1024 + q * 512, part * 1024 + q * 512 + 512)
            value = zown[7, :, cols] + crecv[7, :, cols].astype(jnp.float32)
            value = value + residual[:, cols].astype(jnp.float32)
            for way in (part, 1 - part):
                came = number(way, 1, part, q)
                arrive(rrecv.at[came], r_recv.at[came])
                value = value + rrecv[came].astype(jnp.float32)
            out_ref[:, cols] = jnp.where(alive, value, 0.0).astype(jnp.bfloat16)
    left(xg.at[0:7, 0:32], 0)
    left(xg.at[0:7, 0:32], 1)
    left(xg.at[:, 0:64], 2)
    left(rbuf, 3)
    left(keys, 4)
    left(keys.at[0:128], 5)
    left(heads.at[:, :, 0:384], 6)
    left(csend, 7)
    left(rsend, 8)


def local(hidden_in, spans, w_qkv, w_out):
    bf = jnp.bfloat16
    dma = pltpu.SemaphoreType.DMA
    vmem = pl.BlockSpec(memory_space=pltpu.VMEM)
    anyw = pl.BlockSpec(memory_space=pl.ANY)
    out = pl.pallas_call(
        block_kernel,
        out_shape=jax.ShapeDtypeStruct((64, 2048), bf),
        in_specs=[vmem, anyw, anyw, anyw],
        out_specs=vmem,
        scratch_shapes=[
            pltpu.VMEM((8, 128), jnp.int32),
            pltpu.SMEM((8, 128), jnp.int32),
            pltpu.VMEM((2 * SUBS, 128, UNIT, PIECE), bf),
            pltpu.VMEM((24576, 128), bf),
            pltpu.VMEM((384, 128), jnp.float32),
            pltpu.VMEM((12, 2048, 128), bf),
            pltpu.VMEM((512, 2048), bf),
            pltpu.VMEM((1024, 2048), bf),
            pltpu.VMEM((12, 1024, 128), bf),
            pltpu.VMEM((2, 3, GROUPS, 2, ROWS, 128), bf),
            pltpu.VMEM((2, 3, GROUPS, 3, ROWS, 128), bf),
            pltpu.VMEM((1024, 128), bf),
            pltpu.VMEM((256, UNIT, 128), bf),
            pltpu.VMEM((256, UNIT, 128), bf),
            pltpu.VMEM((2048, 128), bf),
            pltpu.VMEM((2048, 128), bf),
            pltpu.VMEM((8, 128, 2048), bf),
            pltpu.VMEM((8, 128, 1), jnp.float32),
            pltpu.VMEM((8, 128, 512), bf),
            pltpu.VMEM((8, 64, 2048), jnp.float32),
            pltpu.VMEM((8, 64, 2048), bf),
            pltpu.VMEM((8, 64, 2048), bf),
            pltpu.VMEM((28, 64, 512), bf),
            pltpu.VMEM((28, 64, 512), bf),
            dma((4,)), dma((4,)), dma((9,)),
            dma((28,)), dma((28,)), dma((1,)),
            dma((2, 3, GROUPS, 3)), dma((2, 2, GROUPS)), dma((2,)),
            dma((8,)), dma((8,)), dma((28,)),
        ],
        compiler_params=pltpu.CompilerParams(
            collective_id=1, has_side_effects=True, vmem_limit_bytes=60 * 1024 * 1024
        ),
        name="block",
    )(
        spans.T, hidden_in.reshape(8, UNIT, 2048), w_qkv.reshape(24576, 128), w_out.reshape(512, 2048)
    )
    return out[None]


def solution(mesh):
    in_specs = (P("tok", "tp"), P(), P("mod", "tp", None, "tok", None), P("mod", "tok", None, "tp"))
    out_specs = P("mod", "tok", "tp")
    return jax.shard_map(local, mesh=mesh, in_specs=in_specs, out_specs=out_specs, check_vma=False)
```
